128 devices in a mesh: island: 2 (over z_lo), fsdp: 32 (over y, x, z_hi), tensor: 2 (over core).
Axes of the slice: x: 4, y: 4, z: 4 (z_hi: 2, z_lo: 2; z = z_hi * 2 + z_lo), core: 2. Of those that a mesh axis runs over, the one named last changes fastest.
Arguments:
- activations: bfloat16 [65536, 8192], P(('island', 'fsdp'), 'tensor'), may hold values from -6 to 6
- cotangent: bfloat16 [65536, 2, 512], P(('island', 'fsdp'), None, 'tensor'), may hold values from -0.078125 to 0.078125
- inner_params: float32 [2, 8192, 2, 512], P('island', 'fsdp', None, 'tensor'), may hold values from -3 to 3
- first_moment: float32 [2, 8192, 2, 512], P('island', 'fsdp', None, 'tensor'), may hold values from -0.75 to 0.75
- second_moment: float32 [2, 8192, 2, 512], P('island', 'fsdp', None, 'tensor'), may hold values from 0.02 to 0.2
- global_params: float32 [8192, 2, 512], P('fsdp', None, 'tensor'), may hold values from -3 to 3
- outer_momentum: float32 [8192, 2, 512], P('fsdp', None, 'tensor'), may hold values from -1.5 to 1.5
Outputs:
- new_first: float32 [2, 8192, 2, 512], P('island', 'fsdp', None, 'tensor')
- new_second: float32 [2, 8192, 2, 512], P('island', 'fsdp', None, 'tensor')
- new_momentum: float32 [8192, 2, 512], P('fsdp', None, 'tensor')
- new_global: float32 [8192, 2, 512], P('fsdp', None, 'tensor')
- projected: bfloat16 [65536, 2, 512], P(('island', 'fsdp'), None, 'tensor')
The draws below stay inside these ranges and needn't reach their ends.
All inputs are finite; a program needn't handle non-finite values.
Results may differ from the reference program's by a relative error of at most 0.0049.
Values may be sent and summed in bfloat16 or wider, within the bound.
A program may use at most 128 MiB of HBM per device.

```python
import math
import jax
import jax.numpy as jnp
from jax import lax

D = 8192
KV_DIM = 512
TOK_DEV = 1024
STEP = 20
TOKENS = 65536
N_ISLAND = 2
N_FSDP = 32


def level_of(own_key, dims, shards, smallest, largest):
    level = 1.0
    for axis_at, parts in shards:
        heights = jax.random.uniform(jax.random.fold_in(jax.random.fold_in(own_key, 6), axis_at), (parts,), jnp.float32, smallest / len(shards), largest / len(shards))
        level = level * jnp.repeat(jnp.exp(heights), dims[axis_at] // parts).reshape((-1,) + (1,) * (len(dims) - 1 - axis_at))
    return level


def scatter_about(own_key, dims, spread, most, pieces=(), held_as=jnp.bfloat16):
    array = jax.random.normal(own_key, dims, jnp.float32) * spread
    if len(pieces) > 0:
        array = level_of(own_key, dims, pieces, -0.22, 0.18) * array
    return jnp.clip(array, min=-most, max=most).astype(held_as)


def setup_inputs(seed: int = 0) -> dict:
    streams_of = jax.random.split(jax.random.key(seed), 8)
    return {
        "activations": scatter_about(streams_of[0], (TOKENS, D), 1.0, 6.0, ((0, 64), (1, 2))),
        "cotangent": scatter_about(streams_of[1], (TOKENS, 2, KV_DIM), ((TOK_DEV * N_FSDP) ** -0.5), 0.078125, ((0, 64), (2, 2))),
        "inner_params": scatter_about(streams_of[2], (N_ISLAND, D, 2, KV_DIM), 0.2, 3.0, ((0, 2), (1, 32), (3, 2)), jnp.float32),
        "first_moment": scatter_about(streams_of[3], (N_ISLAND, D, 2, KV_DIM), 0.05, 0.75, ((0, 2), (1, 32), (3, 2)), jnp.float32),
        "second_moment": jnp.clip(jnp.exp(math.log(0.2) - 2.3025851 * jax.random.uniform(streams_of[4], (N_ISLAND, D, 2, KV_DIM), jnp.float32) ** level_of(streams_of[4], (N_ISLAND, D, 2, KV_DIM), ((0, 2), (1, 32), (3, 2)), -0.2, 0.2)), 0.02, 0.2),
        "global_params": scatter_about(streams_of[5], (D, 2, KV_DIM), 0.2, 3.0, ((0, 32), (2, 2)), jnp.float32),
        "outer_momentum": scatter_about(streams_of[6], (D, 2, KV_DIM), 0.1, 1.5, ((0, 32), (2, 2)), jnp.float32),
    }


beta_one = 0.9
beta_two = 0.95
adam_eps = 1e-08
inner_rate = 0.05
weight_decay = 0.1
outer_rate = 0.7
outer_mu = 0.9

def replica_gradient(pair):
    rows_x, rows_c = pair

    def add_block(total, block):
        block_x, block_c = block
        part = lax.dot_general(block_x, block_c, (((0,), (0,)), ((), ())), preferred_element_type=jnp.float32)
        return (total + part, None)
    total, _ = lax.scan(add_block, jnp.zeros((D, 2 * KV_DIM), jnp.float32), (rows_x, rows_c))
    return total

def reference(activations, cotangent, inner_params, first_moment, second_moment, global_params, outer_momentum):
    blocks_x = activations.reshape(N_ISLAND, N_FSDP, TOK_DEV, D)
    blocks_c = cotangent.reshape(N_ISLAND, N_FSDP, TOK_DEV, 2 * KV_DIM)
    grad = lax.map(replica_gradient, (blocks_x, blocks_c)).reshape(N_ISLAND, D, 2, KV_DIM)
    new_first = beta_one * first_moment + (1.0 - beta_one) * grad
    new_second = beta_two * second_moment + (1.0 - beta_two) * grad * grad
    ascent = new_first / (1.0 - beta_one ** STEP) / (jnp.sqrt(new_second / (1.0 - beta_two ** STEP)) + adam_eps)
    inner = inner_params - inner_rate * (ascent + weight_decay * inner_params)
    delta = lax.optimization_barrier(jnp.sum(global_params[None] - inner, axis=0)) / N_ISLAND
    new_momentum = outer_mu * outer_momentum + delta
    new_global = global_params - outer_rate * (delta + outer_mu * new_momentum)
    weights = new_global.astype(jnp.bfloat16).reshape(D, 2 * KV_DIM)
    product = jnp.dot(activations, weights, preferred_element_type=jnp.float32) * D ** (-0.5)
    projected = product.reshape(TOKENS, 2, KV_DIM).astype(jnp.bfloat16)
    return (new_first, new_second, new_momentum, new_global, projected)
```

```python
import jax
import jax.numpy as jnp
from jax import lax
from jax.experimental import pallas as pl
from jax.experimental.pallas import tpu as pltpu
from jax.sharding import PartitionSpec as P

D = 8192
STEP = 20
beta_one = 0.9
beta_two = 0.95
adam_eps = 1e-08
inner_rate = 0.05
weight_decay = 0.1
outer_rate = 0.7
outer_mu = 0.9

MESH = pl.DeviceIdType.MESH
bf16 = jnp.bfloat16
f32 = jnp.float32

ORDER = [
    (2, 2), (2, 1), (1, 2), (2, 3), (3, 2), (1, 1), (3, 3), (1, 3),
    (3, 1), (0, 2), (2, 0), (0, 1), (1, 0), (0, 3), (3, 0), (0, 0),
]
ARRIVAL = [
    (0, 0), (0, 1), (1, 0), (0, 3), (3, 0), (0, 2), (2, 0), (1, 1),
    (3, 3), (1, 3), (3, 1), (1, 2), (2, 1), (3, 2), (2, 3), (2, 2),
]


class Numbers:
    def __init__(self):
        self.of = {}

    def __call__(self, key):
        return self.of.setdefault(key, len(self.of))


def kernel(
    count, x_hbm, ct, m_ref, v_ref, th_ref, gp_ref, om_ref,
    nf, ns, nm, ng, out,
    Xc, Pt, A2, Ap, Am, B2, Bp, Bm, Zs, Zr, F, W, Ts, Tr, As, Ar, acc,
    lsem, ssem, rsem,
):
    i = lax.axis_index("island")
    f = lax.axis_index("fsdp")
    t = lax.axis_index("tensor")
    hme = lax.rem(f, 2)
    oh = 1 - hme
    x = lax.rem(lax.div(f, 2), 4)
    y = lax.div(f, 8)

    def wrap(v):
        return lax.rem(v, 4)

    def dev(xx, yy, hh, ii, tt):
        return {"island": ii, "fsdp": (yy * 4 + xx) * 2 + hh, "tensor": tt}

    peer = dev(x, y, hme, i, 1 - t)
    zfar = dev(x, y, oh, i, t)
    zisl = dev(x, y, hme, 1 - i, t)
    zmir = dev(x, y, oh, 1 - i, t)

    def near(axis, s):
        if axis == 0:
            return dev(wrap(x + s), y, hme, i, t)
        return dev(x, wrap(y + s), hme, i, t)

    numbers = Numbers()
    sent = []
    waited = set()

    def message(key, src, dst, to):
        n = numbers(key)
        return pltpu.make_async_remote_copy(
            src_ref=src, dst_ref=dst, send_sem=ssem.at[n], recv_sem=rsem.at[n],
            device_id=to, device_id_type=MESH,
        )

    def send(key, src, dst, to):
        message(key, src, dst, to).start()
        sent.append((key, src, dst, to))

    def recv(key, dst):
        if key not in waited:
            waited.add(key)
            message(key, dst, dst, peer).wait_recv()

    barrier = pltpu.get_barrier_semaphore()
    friends = [near(0, 1), near(0, 3), near(1, 1), near(1, 3), peer, zfar, zisl, zmir]
    for d in friends:
        pl.semaphore_signal(barrier, inc=1, device_id=d, device_id_type=MESH)

    def place(p, ja, jb):
        dx, dy = (ja, jb) if p == 0 else (jb, ja)
        return wrap(y + dy), wrap(x + dx)

    def chunk(c):
        dy, dx = ORDER[c]
        yy, xx = wrap(y + dy), wrap(x + dx)
        k = yy * 4 + xx
        mine = lax.div(yy, 2) == t
        src = x_hbm.at[:, pl.ds(pl.multiple_of(lax.rem(k, 8) * 512, 512), 512)]
        return k, mine, src

    for c in range(16):
        k, mine, src = chunk(c)

        @pl.when(mine)
        def _():
            pltpu.make_async_copy(src, Xc.at[k], lsem.at[c]).start()

    pl.semaphore_wait(barrier, len(friends))
    for c in range(16):
        k, mine, src = chunk(c)
        n = numbers(("X", c))

        @pl.when(mine)
        def _():
            message(("X", c), src, Xc.at[k], peer).start()

    def gradient(c):
        k, mine, src = chunk(c)

        @pl.when(mine)
        def _():
            pltpu.make_async_copy(src, Xc.at[k], lsem.at[c]).wait()

        @pl.when(jnp.logical_not(mine))
        def _():
            message(("X", c), Xc.at[k], Xc.at[k], peer).wait_recv()

        dy, dx = ORDER[c]
        yy, xx = wrap(y + dy), wrap(x + dx)
        for h in range(2):
            part = jnp.dot(
                ct[...], Xc[k, :, h * 256 : (h + 1) * 256], preferred_element_type=f32
            ).astype(bf16)
            for u in range(2):
                for p in range(2):
                    r = (u * 2 + p) * 128
                    Pt[u, p, yy, xx, h] = part[r : r + 128]

    def Pc(u, p, ja, jb, h):
        yy, xx = place(p, ja, jb)
        return Pt.at[u, p, yy, xx, h]

    def first_sends(u, c):
        dy, dx = ORDER[c]
        for p in range(2):
            a = p
            ja, jb = (dx, dy) if p == 0 else (dy, dx)
            if ja == 2:
                send(("A2", u, p, jb, 0), Pc(u, p, 2, jb, 0), A2.at[u, p, jb, 0], near(a, 1))
                send(("A2", u, p, jb, 1), Pc(u, p, 2, jb, 1), A2.at[u, p, jb, 1], near(a, 3))
            elif ja == 1:
                send(("Am", u, p, jb, 1), Pc(u, p, 1, jb, 1), Am.at[u, p, jb, 1], near(a, 1))
            elif ja == 3:
                send(("Ap", u, p, jb, 0), Pc(u, p, 3, jb, 0), Ap.at[u, p, jb, 0], near(a, 3))

    def add_to(dst, src):
        dst[...] = (dst[...].astype(f32) + src[...].astype(f32)).astype(bf16)

    def rs1b(u, jb):
        for p in range(2):
            a = p
            recv(("A2", u, p, jb, 0), A2.at[u, p, jb, 0])
            add_to(Pc(u, p, 1, jb, 0), A2.at[u, p, jb, 0])
            send(("Am", u, p, jb, 0), Pc(u, p, 1, jb, 0), Am.at[u, p, jb, 0], near(a, 1))
            recv(("A2", u, p, jb, 1), A2.at[u, p, jb, 1])
            add_to(Pc(u, p, 3, jb, 1), A2.at[u, p, jb, 1])
            send(("Ap", u, p, jb, 1), Pc(u, p, 3, jb, 1), Ap.at[u, p, jb, 1], near(a, 3))

    def rs1c(u, jb):
        for p in range(2):
            b = 1 - p
            for h in range(2):
                recv(("Am", u, p, jb, h), Am.at[u, p, jb, h])
                recv(("Ap", u, p, jb, h), Ap.at[u, p, jb, h])
                own = Pc(u, p, 0, jb, h)
                s = own[...].astype(f32) + Am[u, p, jb, h].astype(f32) + Ap[u, p, jb, h].astype(f32)
                if jb == 0:
                    F[u, p, h] = s
                else:
                    own[...] = s.astype(bf16)
                    if jb == 2:
                        send(("B2", u, p, h), own, B2.at[u, p, h], near(b, 1 if h == 0 else 3))
                    elif jb == 1 and h == 1:
                        send(("Bm", u, p, 1), own, Bm.at[u, p, 1], near(b, 1))
                    elif jb == 3 and h == 0:
                        send(("Bp", u, p, 0), own, Bp.at[u, p, 0], near(b, 3))

    def rs2b(u):
        for p in range(2):
            b = 1 - p
            recv(("B2", u, p, 0), B2.at[u, p, 0])
            add_to(Pc(u, p, 0, 1, 0), B2.at[u, p, 0])
            send(("Bm", u, p, 0), Pc(u, p, 0, 1, 0), Bm.at[u, p, 0], near(b, 1))
            recv(("B2", u, p, 1), B2.at[u, p, 1])
            add_to(Pc(u, p, 0, 3, 1), B2.at[u, p, 1])
            send(("Bp", u, p, 1), Pc(u, p, 0, 3, 1), Bp.at[u, p, 1], near(b, 3))

    def rs2c(u):
        for p in range(2):
            for h in range(2):
                recv(("Bm", u, p, h), Bm.at[u, p, h])
                recv(("Bp", u, p, h), Bp.at[u, p, h])
                F[u, p, h] += Bm[u, p, h].astype(f32) + Bp[u, p, h].astype(f32)
            Zs[u, p] = F[u, p, oh].astype(bf16)
            send(("Z", u, p), Zs.at[u, p], Zr.at[u, p], zfar)

    def start_islands():
        for u in range(2):
            th = th_ref[:, u, :]
            Ts[u] = gp_ref[:, u, :] - (th - (inner_rate * weight_decay) * th)
        send(("T",), Ts, Tr, zisl)

    def adam(u):
        for p in range(2):
            cols = slice(p * 128, (p + 1) * 128)
            recv(("Z", u, p), Zr.at[u, p])
            grad = (F[u, p, hme] + Zr[u, p].astype(f32)).T
            first = beta_one * m_ref[:, u, cols] + (1.0 - beta_one) * grad
            second = beta_two * v_ref[:, u, cols] + (1.0 - beta_two) * grad * grad
            nf[:, u, cols] = first
            ns[:, u, cols] = second
            ascent = (
                first / (1.0 - beta_one**STEP)
                / (jnp.sqrt(second / (1.0 - beta_two**STEP)) + adam_eps)
            )
            As[u, p] = ascent.astype(bf16)
            send(("I", u, p), As.at[u, p], Ar.at[u, p], zisl)

    def Wp(u, p, ja, jb):
        yy, xx = place(p, ja, jb)
        return W.at[u, yy, xx, :, p]

    def Wh(u, p, ja, jb, h):
        yy, xx = place(p, ja, jb)
        return W.at[u, yy, xx, h, p]

    def outer(u):
        recv(("T",), Tr)
        for p in range(2):
            cols = slice(p * 128, (p + 1) * 128)
            recv(("I", u, p), Ar.at[u, p])
            steps = As[u, p].astype(f32) + Ar[u, p].astype(f32)
            delta = ((Ts[u, :, cols] + Tr[u, :, cols]) + inner_rate * steps) * 0.5
            momentum = outer_mu * om_ref[:, u, cols] + delta
            fresh = gp_ref[:, u, cols] - outer_rate * (delta + outer_mu * momentum)
            nm[:, u, cols] = momentum
            ng[:, u, cols] = fresh
            low = fresh.astype(bf16)
            W[u, y, x, hme, 0, :, cols] = low[:128]
            W[u, y, x, hme, 1, :, cols] = low[128:]
        send(("Gz", u), W.at[u, y, x, hme], W.at[u, y, x, hme], zmir)
        spread(u, 0)

    def spread(u, s):
        h = hme if s == 0 else oh
        for p in range(2):
            for g in (1, 3):
                ref = Wh(u, p, 0, 0, h)
                send(("G1", u, p, s, g), ref, ref, near(p, g))
                send(("G2", u, p, 0, s, g), ref, ref, near(1 - p, g))

    def agz(u):
        recv(("Gz", u), W.at[u, y, x, oh])
        spread(u, 1)

    def g2(u, p, j):
        for g in (1, 3):
            ref = Wp(u, p, j, 0)
            send(("G2", u, p, j, g), ref, ref, near(1 - p, g))

    def ag1(u):
        for p in range(2):
            recv(("G1", u, p, 0, 1), Wh(u, p, 3, 0, hme))
            ref = Wh(u, p, 3, 0, hme)
            send(("G1f", u, p, 1), ref, ref, near(p, 1))
            recv(("G1", u, p, 1, 3), Wh(u, p, 1, 0, oh))
            ref = Wh(u, p, 1, 0, oh)
            send(("G1f", u, p, 3), ref, ref, near(p, 3))
        for p in range(2):
            recv(("G1", u, p, 1, 1), Wh(u, p, 3, 0, oh))
            g2(u, p, 3)
            recv(("G1", u, p, 0, 3), Wh(u, p, 1, 0, hme))
            g2(u, p, 1)

    def ag1f(u):
        for p in range(2):
            recv(("G1f", u, p, 1), Wh(u, p, 2, 0, hme))
            recv(("G1f", u, p, 3), Wh(u, p, 2, 0, oh))
            g2(u, p, 2)

    def ag2f(u, j):
        for p in range(2):
            if j == 0:
                recv(("G2", u, p, 0, 0, 1), Wh(u, p, 0, 3, hme))
            else:
                recv(("G2", u, p, j, 1), Wp(u, p, j, 3))
            ref = Wh(u, p, j, 3, hme)
            send(("G2f", u, p, j, 1), ref, ref, near(1 - p, 1))
            if j == 0:
                recv(("G2", u, p, 0, 1, 3), Wh(u, p, 0, 1, oh))
            else:
                recv(("G2", u, p, j, 3), Wp(u, p, j, 1))
            ref = Wh(u, p, j, 1, oh)
            send(("G2f", u, p, j, 3), ref, ref, near(1 - p, 3))

    seen = set()

    def project(u, c):
        dy, dx = ARRIVAL[c]
        for p in range(2):
            ja, jb = (dx, dy) if p == 0 else (dy, dx)
            if jb == 3 and ja == 0:
                recv(("G2", u, p, 0, 1, 1), Wh(u, p, 0, 3, oh))
            if jb == 1 and ja == 0:
                recv(("G2", u, p, 0, 0, 3), Wh(u, p, 0, 1, hme))
            if jb == 2:
                recv(("G2f", u, p, ja, 1), Wh(u, p, ja, 2, hme))
                recv(("G2f", u, p, ja, 3), Wh(u, p, ja, 2, oh))
        yy, xx = wrap(y + dy), wrap(x + dx)
        right = W[u, yy, xx].reshape(512, 256)
        part = jnp.dot(Xc[yy * 4 + xx], right, preferred_element_type=f32)
        cols = slice(u * 256, (u + 1) * 256)
        if u not in seen:
            seen.add(u)
            acc[:, cols] = part
        elif c < 15:
            acc[:, cols] += part
        else:
            out[:, cols] = ((acc[:, cols] + part) * D ** (-0.5)).astype(bf16)

    for c in range(16):
        gradient(c)
        first_sends(0, c)
        if c == 6:
            start_islands()
    for q, jb in enumerate((2, 1, 3, 0)):
        rs1b(0, jb)
        for c in range(4 * q, 4 * q + 4):
            first_sends(1, c)
    for jb in (2, 1, 3, 0):
        rs1c(0, jb)
    rs2b(0)
    rs1b(1, 2)
    rs2c(0)
    rs1b(1, 1)
    adam(0)
    rs1b(1, 3)
    rs1b(1, 0)
    outer(0)
    rs1c(1, 2)
    agz(0)
    rs1c(1, 1)
    ag1(0)
    rs1c(1, 3)
    ag1f(0)
    rs1c(1, 0)
    ag2f(0, 0)
    rs2b(1)
    ag2f(0, 3)
    rs2c(1)
    ag2f(0, 1)
    adam(1)
    ag2f(0, 2)
    outer(1)
    for c in range(0, 5):
        project(0, c)
    agz(1)
    for c in range(5, 9):
        project(0, c)
    ag1(1)
    for c in range(9, 12):
        project(0, c)
    ag1f(1)
    for c in range(12, 16):
        project(0, c)
    ag2f(1, 0)
    project(1, 0)
    project(1, 1)
    ag2f(1, 3)
    project(1, 2)
    project(1, 3)
    ag2f(1, 1)
    project(1, 4)
    ag2f(1, 2)
    for c in range(5, 16):
        project(1, c)

    for key, src, dst, to in sent:
        message(key, src, dst, to).wait_send()
    for c in range(16):
        k, mine, src = chunk(c)

        @pl.when(mine)
        def _():
            message(("X", c), src, Xc.at[k], peer).wait_send()

    if len(numbers.of) != count:
        raise ValueError(len(numbers.of))


COUNT = 243


def shards(
    activations, cotangent, inner_params, first_moment, second_moment, global_params, outer_momentum
):
    tok, kv = cotangent.shape[0], cotangent.shape[2]
    rows = global_params.shape[0]
    ct = cotangent.reshape(tok, 2 * kv).T
    vmem = pl.BlockSpec(memory_space=pltpu.VMEM)
    state = jax.ShapeDtypeStruct((rows, 2, kv), f32)
    import functools

    piece = (128, 256)
    new_first, new_second, new_momentum, new_global, projected = pl.pallas_call(
        functools.partial(kernel, COUNT),
        out_shape=(state, state, state, state, jax.ShapeDtypeStruct((tok, 2 * kv), bf16)),
        in_specs=[pl.BlockSpec(memory_space=pl.ANY)] + [vmem] * 6,
        out_specs=(vmem,) * 5,
        scratch_shapes=[
            pltpu.VMEM((16, tok, 512), bf16),
            pltpu.VMEM((2, 2, 4, 4, 2) + piece, bf16),
            pltpu.VMEM((2, 2, 4, 2) + piece, bf16),
            pltpu.VMEM((2, 2, 4, 2) + piece, bf16),
            pltpu.VMEM((2, 2, 4, 2) + piece, bf16),
            pltpu.VMEM((2, 2, 2) + piece, bf16),
            pltpu.VMEM((2, 2, 2) + piece, bf16),
            pltpu.VMEM((2, 2, 2) + piece, bf16),
            pltpu.VMEM((2, 2) + piece, bf16),
            pltpu.VMEM((2, 2) + piece, bf16),
            pltpu.VMEM((2, 2, 2) + piece, f32),
            pltpu.VMEM((2, 4, 4, 2, 2) + piece, bf16),
            pltpu.VMEM((2, rows, kv), f32),
            pltpu.VMEM((2, rows, kv), f32),
            pltpu.VMEM((2, 2, rows, kv // 2), bf16),
            pltpu.VMEM((2, 2, rows, kv // 2), bf16),
            pltpu.VMEM((tok, 2 * kv), f32),
            pltpu.SemaphoreType.DMA((16,)),
            pltpu.SemaphoreType.DMA((COUNT,)),
            pltpu.SemaphoreType.DMA((COUNT,)),
        ],
        compiler_params=pltpu.CompilerParams(
            collective_id=0, has_side_effects=True, vmem_limit_bytes=62 * 2**20
        ),
        cost_estimate=pl.CostEstimate(
            flops=17_200_000_000, bytes_accessed=16 * 2**20, transcendentals=0
        ),
        name="outer_step",
    )(
        activations, ct, first_moment[0], second_moment[0], inner_params[0],
        global_params, outer_momentum,
    )
    return (
        new_first[None], new_second[None], new_momentum, new_global,
        projected.reshape(tok, 2, kv),
    )


def solution(mesh):
    in_specs = (
        P(("island", "fsdp"), "tensor"),
        P(("island", "fsdp"), None, "tensor"),
        P("island", "fsdp", None, "tensor"),
        P("island", "fsdp", None, "tensor"),
        P("island", "fsdp", None, "tensor"),
        P("fsdp", None, "tensor"),
        P("fsdp", None, "tensor"),
    )
    out_specs = (
        P("island", "fsdp", None, "tensor"),
        P("island", "fsdp", None, "tensor"),
        P("fsdp", None, "tensor"),
        P("fsdp", None, "tensor"),
        P(("island", "fsdp"), None, "tensor"),
    )
    return jax.shard_map(shards, mesh=mesh, in_specs=in_specs, out_specs=out_specs, check_vma=False)
```

```python
import functools

import jax
import jax.numpy as jnp
from jax import lax
from jax.experimental import pallas as pl
from jax.experimental.pallas import tpu as pltpu
from jax.sharding import PartitionSpec as P

D = 8192
STEP = 20
beta_one = 0.9
beta_two = 0.95
adam_eps = 1e-08
inner_rate = 0.05
weight_decay = 0.1
outer_rate = 0.7
outer_mu = 0.9

MESH = pl.DeviceIdType.MESH
bf16 = jnp.bfloat16
f32 = jnp.float32

ORDER = [
    (2, 2), (2, 1), (1, 2), (2, 3), (3, 2), (1, 1), (3, 3), (1, 3),
    (3, 1), (0, 2), (2, 0), (0, 1), (1, 0), (0, 3), (3, 0), (0, 0),
]
ARRIVAL = [
    (0, 0), (0, 1), (1, 0), (0, 3), (3, 0), (0, 2), (2, 0), (1, 1),
    (3, 3), (1, 3), (3, 1), (1, 2), (2, 1), (3, 2), (2, 3), (2, 2),
]


class Numbers:
    def __init__(self):
        self.of = {}

    def __call__(self, key):
        return self.of.setdefault(key, len(self.of))


def kernel(
    count, x_hbm, c_hbm, m_hbm, v_hbm, th_hbm, gp_hbm, om_hbm,
    nf_hbm, ns_hbm, nm_hbm, ng_hbm, out_hbm,
    cot, ct, m_ref, v_ref, th_ref, gp_ref, om_ref, nf, ns, nm, ng, out,
    Xc, Pt, A2, Ap, Am, B2, Bp, Bm, Zs, Zr, F, W, Ts, Tr, As, Ar, acc,
    lsem, ssem, rsem,
):
    i = lax.axis_index("island")
    f = lax.axis_index("fsdp")
    t = lax.axis_index("tensor")
    hme = lax.rem(f, 2)
    oh = 1 - hme
    x = lax.rem(lax.div(f, 2), 4)
    y = lax.div(f, 8)

    def wrap(v):
        return lax.rem(v, 4)

    def dev(xx, yy, hh, ii, tt):
        return {"island": ii, "fsdp": (yy * 4 + xx) * 2 + hh, "tensor": tt}

    peer = dev(x, y, hme, i, 1 - t)
    zfar = dev(x, y, oh, i, t)
    zisl = dev(x, y, hme, 1 - i, t)
    zmir = dev(x, y, oh, 1 - i, t)

    sense = 1 + 2 * i

    def near(axis, s):
        if axis == 0:
            return dev(wrap(x + s), y, hme, i, t)
        return dev(x, wrap(y + s), hme, i, t)

    numbers = Numbers()
    sent = []
    waited = set()

    def message(key, src, dst, to):
        n = numbers(key)
        return pltpu.make_async_remote_copy(
            src_ref=src, dst_ref=dst, send_sem=ssem.at[n], recv_sem=rsem.at[n],
            device_id=to, device_id_type=MESH,
        )

    def send(key, src, dst, to):
        message(key, src, dst, to).start()
        sent.append((key, src, dst, to))

    def recv(key, dst):
        if key not in waited:
            waited.add(key)
            message(key, dst, dst, peer).wait_recv()

    barrier = pltpu.get_barrier_semaphore()
    friends = [near(0, 1), near(0, 3), near(1, 1), near(1, 3), peer, zfar, zisl, zmir]
    for d in friends:
        pl.semaphore_signal(barrier, inc=1, device_id=d, device_id_type=MESH)

    state_in = [
        pltpu.make_async_copy(a, b, lsem.at[16 + n])
        for n, (a, b) in enumerate((
            (c_hbm, cot), (th_hbm, th_ref), (gp_hbm, gp_ref),
            (m_hbm, m_ref), (v_hbm, v_ref), (om_hbm, om_ref),
        ))
    ]
    state_in[0].start()

    def place(p, ja, jb):
        dx, dy = (ja, jb) if p == 0 else (jb, ja)
        return wrap(y + dy), wrap(x + dx)

    def chunk(c):
        dy, dx = ORDER[c]
        yy, xx = wrap(y + dy), wrap(x + dx)
        k = yy * 4 + xx
        mine = lax.div(yy, 2) == t
        src = x_hbm.at[:, pl.ds(pl.multiple_of(lax.rem(k, 8) * 512, 512), 512)]
        return k, mine, src

    for c in range(16):
        k, mine, src = chunk(c)

        @pl.when(mine)
        def _():
            pltpu.make_async_copy(src, Xc.at[k], lsem.at[c]).start()

    for copy in state_in[1:]:
        copy.start()
    state_in[0].wait()
    for u in range(2):
        ct[u * 256 : (u + 1) * 256, :] = cot[:, u, :].T

    pl.semaphore_wait(barrier, len(friends))
    for c in range(16):
        k, mine, src = chunk(c)
        n = numbers(("X", c))

        @pl.when(mine)
        def _():
            message(("X", c), src, Xc.at[k], peer).start()

    def gradient(c):
        k, mine, src = chunk(c)

        @pl.when(mine)
        def _():
            pltpu.make_async_copy(src, Xc.at[k], lsem.at[c]).wait()

        @pl.when(jnp.logical_not(mine))
        def _():
            message(("X", c), Xc.at[k], Xc.at[k], peer).wait_recv()

        dy, dx = ORDER[c]
        yy, xx = wrap(y + dy), wrap(x + dx)
        for h in range(2):
            part = jnp.dot(
                ct[...], Xc[k, :, h * 256 : (h + 1) * 256], preferred_element_type=f32
            ).astype(bf16)
            for u in range(2):
                for p in range(2):
                    r = (u * 2 + p) * 128
                    Pt[u, p, yy, xx, h] = part[r : r + 128]

    def Pc(u, p, ja, jb, h):
        yy, xx = place(p, ja, jb)
        return Pt.at[u, p, yy, xx, h]

    def first_sends(u, c):
        dy, dx = ORDER[c]
        for p in range(2):
            a = p
            ja, jb = (dx, dy) if p == 0 else (dy, dx)
            if ja == 2:
                send(("A2", u, p, jb, 0), Pc(u, p, 2, jb, 0), A2.at[u, p, jb, 0], near(a, 1))
                send(("A2", u, p, jb, 1), Pc(u, p, 2, jb, 1), A2.at[u, p, jb, 1], near(a, 3))
            elif ja == 1:
                send(("Am", u, p, jb, 1), Pc(u, p, 1, jb, 1), Am.at[u, p, jb, 1], near(a, 1))
            elif ja == 3:
                send(("Ap", u, p, jb, 0), Pc(u, p, 3, jb, 0), Ap.at[u, p, jb, 0], near(a, 3))

    def add_to(dst, src):
        dst[...] = (dst[...].astype(f32) + src[...].astype(f32)).astype(bf16)

    def rs1b(u, jb):
        for p in range(2):
            a = p
            recv(("A2", u, p, jb, 0), A2.at[u, p, jb, 0])
            add_to(Pc(u, p, 1, jb, 0), A2.at[u, p, jb, 0])
            send(("Am", u, p, jb, 0), Pc(u, p, 1, jb, 0), Am.at[u, p, jb, 0], near(a, 1))
            recv(("A2", u, p, jb, 1), A2.at[u, p, jb, 1])
            add_to(Pc(u, p, 3, jb, 1), A2.at[u, p, jb, 1])
            send(("Ap", u, p, jb, 1), Pc(u, p, 3, jb, 1), Ap.at[u, p, jb, 1], near(a, 3))

    def rs1c(u, jb):
        for p in range(2):
            b = 1 - p
            for h in range(2):
                recv(("Am", u, p, jb, h), Am.at[u, p, jb, h])
                recv(("Ap", u, p, jb, h), Ap.at[u, p, jb, h])
                own = Pc(u, p, 0, jb, h)
                s = own[...].astype(f32) + Am[u, p, jb, h].astype(f32) + Ap[u, p, jb, h].astype(f32)
                if jb == 0:
                    F[u, p, h] = s
                else:
                    own[...] = s.astype(bf16)
                    if jb == 2:
                        send(("B2", u, p, h), own, B2.at[u, p, h], near(b, 1 if h == 0 else 3))
                    elif jb == 1 and h == 1:
                        send(("Bm", u, p, 1), own, Bm.at[u, p, 1], near(b, 1))
                    elif jb == 3 and h == 0:
                        send(("Bp", u, p, 0), own, Bp.at[u, p, 0], near(b, 3))

    def rs2b(u):
        for p in range(2):
            b = 1 - p
            recv(("B2", u, p, 0), B2.at[u, p, 0])
            add_to(Pc(u, p, 0, 1, 0), B2.at[u, p, 0])
            send(("Bm", u, p, 0), Pc(u, p, 0, 1, 0), Bm.at[u, p, 0], near(b, 1))
            recv(("B2", u, p, 1), B2.at[u, p, 1])
            add_to(Pc(u, p, 0, 3, 1), B2.at[u, p, 1])
            send(("Bp", u, p, 1), Pc(u, p, 0, 3, 1), Bp.at[u, p, 1], near(b, 3))

    def rs2c(u):
        for p in range(2):
            for h in range(2):
                recv(("Bm", u, p, h), Bm.at[u, p, h])
                recv(("Bp", u, p, h), Bp.at[u, p, h])
                F[u, p, h] += Bm[u, p, h].astype(f32) + Bp[u, p, h].astype(f32)
            Zs[u, p] = F[u, p, oh].astype(bf16)
            send(("Z", u, p), Zs.at[u, p], Zr.at[u, p], zfar)

    def start_islands():
        for copy in state_in[1:]:
            copy.wait()
        for u in range(2):
            th = th_ref[:, u, :]
            Ts[u] = gp_ref[:, u, :] - (th - (inner_rate * weight_decay) * th)
        send(("T",), Ts, Tr, zisl)

    def adam(u):
        for p in range(2):
            cols = slice(p * 128, (p + 1) * 128)
            recv(("Z", u, p), Zr.at[u, p])
            grad = (F[u, p, hme] + Zr[u, p].astype(f32)).T
            first = beta_one * m_ref[:, u, cols] + (1.0 - beta_one) * grad
            second = beta_two * v_ref[:, u, cols] + (1.0 - beta_two) * grad * grad
            nf[:, u, cols] = first
            ns[:, u, cols] = second
            ascent = (
                first / (1.0 - beta_one**STEP)
                / (jnp.sqrt(second / (1.0 - beta_two**STEP)) + adam_eps)
            )
            As[u, p] = ascent.astype(bf16)
            send(("I", u, p), As.at[u, p], Ar.at[u, p], zisl)

    def place_w(p, ja, jb):
        return place(p, sense * ja, sense * jb)

    def near_w(axis, g):
        return near(axis, sense * g)

    def Wp(u, p, ja, jb):
        yy, xx = place_w(p, ja, jb)
        return W.at[u, yy, xx, :, p]

    def Wh(u, p, ja, jb, h):
        yy, xx = place_w(p, ja, jb)
        return W.at[u, yy, xx, h, p]

    def outer(u):
        recv(("T",), Tr)
        for p in range(2):
            cols = slice(p * 128, (p + 1) * 128)
            recv(("I", u, p), Ar.at[u, p])
            steps = As[u, p].astype(f32) + Ar[u, p].astype(f32)
            delta = ((Ts[u, :, cols] + Tr[u, :, cols]) + inner_rate * steps) * 0.5
            momentum = outer_mu * om_ref[:, u, cols] + delta
            fresh = gp_ref[:, u, cols] - outer_rate * (delta + outer_mu * momentum)
            nm[:, u, cols] = momentum
            ng[:, u, cols] = fresh
            low = fresh.astype(bf16)
            W[u, y, x, hme, 0, :, cols] = low[:128]
            W[u, y, x, hme, 1, :, cols] = low[128:]
        send(("Gz", u), W.at[u, y, x, hme], W.at[u, y, x, hme], zmir)
        spread(u, 0)

    def spread(u, s):
        h = hme if s == 0 else oh
        for p in range(2):
            ref = Wh(u, p, 0, 0, h)
            for g in (1, 3):
                send(("G1", u, p, s, g), ref, ref, near_w(p, g))
            send(("G2b", u, p, 0, s), ref, ref, near_w(1 - p, 3))

            @pl.when(h == i)
            def _():
                message(("G2e", u, p, 0), ref, ref, near_w(1 - p, 1)).start()

            if s == 1:
                own = Wh(u, p, 0, 0, i)
                sent.append((("G2e", u, p, 0), own, own, near_w(1 - p, 1)))

    def agz(u):
        recv(("Gz", u), W.at[u, y, x, oh])
        spread(u, 1)

    def g2(u, p, j):
        ref = Wh(u, p, j, 0, i)
        send(("G2e", u, p, j), ref, ref, near_w(1 - p, 1))
        ref = Wp(u, p, j, 0)
        send(("G2b", u, p, j), ref, ref, near_w(1 - p, 3))

    def ag1(u):
        for p in range(2):
            ref = Wh(u, p, 3, 0, hme)
            recv(("G1", u, p, 0, 1), ref)
            send(("G1f", u, p, 1), ref, ref, near_w(p, 1))
            ref = Wh(u, p, 1, 0, oh)
            recv(("G1", u, p, 1, 3), ref)
            send(("G1f", u, p, 3), ref, ref, near_w(p, 3))
        for p in range(2):
            recv(("G1", u, p, 1, 1), Wh(u, p, 3, 0, oh))
            g2(u, p, 3)
            recv(("G1", u, p, 0, 3), Wh(u, p, 1, 0, hme))
            g2(u, p, 1)

    def ag1f(u):
        for p in range(2):
            recv(("G1f", u, p, 1), Wh(u, p, 2, 0, hme))
            recv(("G1f", u, p, 3), Wh(u, p, 2, 0, oh))
            g2(u, p, 2)

    def ahead(u, p, j):
        if j == 0:
            recv(("G2b", u, p, 0, 0), Wh(u, p, 0, 1, hme))
            recv(("G2b", u, p, 0, 1), Wh(u, p, 0, 1, oh))
        else:
            recv(("G2b", u, p, j), Wp(u, p, j, 1))

    def ag2f(u, j):
        for p in range(2):
            ref = Wh(u, p, j, 3, i)
            recv(("G2e", u, p, j), ref)
            send(("G2f", u, p, j), ref, ref, near_w(1 - p, 1))
        for p in range(2):
            ahead(u, p, j)
            ref = Wh(u, p, j, 1, i)
            send(("G2m", u, p, (4 - j) % 4), ref, ref, zmir)

    def ag2z(u, j):
        for p in range(2):
            ref = Wh(u, p, j, 2, i)
            recv(("G2f", u, p, j), ref)
            send(("G2z", u, p, (4 - j) % 4), ref, ref, zisl)

    leaving = []

    def leave(n, src, dst):
        copy = pltpu.make_async_copy(src, dst, lsem.at[22 + n])
        copy.start()
        leaving.append(copy)

    seen = set()

    def project(u, c):
        dy, dx = ARRIVAL[c]
        for p in range(2):
            ja, jb = (dx, dy) if p == 0 else (dy, dx)
            if jb == 1:
                ahead(u, p, ja)
            if jb == 3:
                recv(("G2e", u, p, ja), Wh(u, p, ja, 3, i))
                recv(("G2m", u, p, ja), Wh(u, p, ja, 3, 1 - i))
            if jb == 2:
                recv(("G2f", u, p, ja), Wh(u, p, ja, 2, i))
                recv(("G2z", u, p, ja), Wh(u, p, ja, 2, 1 - i))
        yy, xx = wrap(y + sense * dy), wrap(x + sense * dx)
        right = W[u, yy, xx].reshape(512, 256)
        part = jnp.dot(Xc[yy * 4 + xx], right, preferred_element_type=f32)
        cols = slice(u * 256, (u + 1) * 256)
        if u not in seen:
            seen.add(u)
            acc[:, cols] = part
        elif c < 15:
            acc[:, cols] += part
        else:
            out[:, cols] = ((acc[:, cols] + part) * D ** (-0.5)).astype(bf16)
            leave(4 + u, out.at[:, cols], out_hbm.at[:, cols])

    for c in range(16):
        gradient(c)
        first_sends(0, c)
        if c == 6:
            start_islands()
    for q, jb in enumerate((2, 1, 3, 0)):
        rs1b(0, jb)
        for c in range(4 * q, 4 * q + 4):
            first_sends(1, c)
    for jb in (2, 1, 3, 0):
        rs1c(0, jb)
    rs2b(0)
    rs1b(1, 2)
    rs2c(0)
    rs1b(1, 1)
    adam(0)
    rs1b(1, 3)
    rs1b(1, 0)
    outer(0)
    rs1c(1, 2)
    agz(0)
    rs1c(1, 1)
    rs1c(1, 3)
    ag1(0)
    rs1c(1, 0)
    rs2b(1)
    ag1f(0)
    ag2f(0, 0)
    rs2c(1)
    ag2f(0, 3)
    ag2f(0, 1)
    adam(1)
    leave(0, nf, nf_hbm)
    leave(1, ns, ns_hbm)
    ag2z(0, 0)
    ag2f(0, 2)
    outer(1)
    leave(2, nm, nm_hbm)
    leave(3, ng, ng_hbm)
    ag2z(0, 3)
    ag2z(0, 1)
    for c in range(0, 3):
        project(0, c)
    agz(1)
    ag2z(0, 2)
    for c in range(3, 6):
        project(0, c)
    ag1(1)
    for c in range(6, 10):
        project(0, c)
    ag1f(1)
    for c in range(10, 12):
        project(0, c)
    ag2f(1, 0)
    for c in range(12, 14):
        project(0, c)
    ag2f(1, 3)
    ag2f(1, 1)
    for c in range(14, 16):
        project(0, c)
    ag2z(1, 0)
    project(1, 0)
    ag2f(1, 2)
    project(1, 1)
    project(1, 2)
    ag2z(1, 3)
    project(1, 3)
    ag2z(1, 1)
    project(1, 4)
    ag2z(1, 2)
    for c in range(5, 16):
        project(1, c)

    for copy in leaving:
        copy.wait()
    for key, src, dst, to in sent:
        message(key, src, dst, to).wait_send()
    for c in range(16):
        k, mine, src = chunk(c)

        @pl.when(mine)
        def _():
            message(("X", c), src, Xc.at[k], peer).wait_send()

    if len(numbers.of) != count:
        raise ValueError(len(numbers.of))


COUNT = 255


def hand_over(*refs):
    ins, outs, held, sem = refs[:4], refs[4:8], refs[8:12], refs[12]
    there = [pltpu.make_async_copy(a, b, sem.at[n]) for n, (a, b) in enumerate(zip(ins, held))]
    back = [pltpu.make_async_copy(a, b, sem.at[4 + n]) for n, (a, b) in enumerate(zip(held, outs))]
    for copy in there:
        copy.start()
    for first, second in zip(there, back):
        first.wait()
        second.start()
    for copy in back:
        copy.wait()


def shards(
    activations, cotangent, inner_params, first_moment, second_moment, global_params, outer_momentum
):
    tok, kv = cotangent.shape[0], cotangent.shape[2]
    rows = global_params.shape[0]
    anywhere = pl.BlockSpec(memory_space=pl.ANY)
    state = jax.ShapeDtypeStruct((rows, 2, kv), f32)
    piece = (128, 256)
    held = pltpu.VMEM((rows, 2, kv), f32)
    *states, projected = pl.pallas_call(
        functools.partial(kernel, COUNT),
        out_shape=(state, state, state, state, jax.ShapeDtypeStruct((tok, 2 * kv), bf16)),
        in_specs=[anywhere] * 7,
        out_specs=(anywhere,) * 5,
        scratch_shapes=[
            pltpu.VMEM((tok, 2, kv), bf16),
            pltpu.VMEM((2 * kv, tok), bf16),
            held, held, held, held, held, held, held, held, held,
            pltpu.VMEM((tok, 2 * kv), bf16),
            pltpu.VMEM((16, tok, 512), bf16),
            pltpu.VMEM((2, 2, 4, 4, 2) + piece, bf16),
            pltpu.VMEM((2, 2, 4, 2) + piece, bf16),
            pltpu.VMEM((2, 2, 4, 2) + piece, bf16),
            pltpu.VMEM((2, 2, 4, 2) + piece, bf16),
            pltpu.VMEM((2, 2, 2) + piece, bf16),
            pltpu.VMEM((2, 2, 2) + piece, bf16),
            pltpu.VMEM((2, 2, 2) + piece, bf16),
            pltpu.VMEM((2, 2) + piece, bf16),
            pltpu.VMEM((2, 2) + piece, bf16),
            pltpu.VMEM((2, 2, 2) + piece, f32),
            pltpu.VMEM((2, 4, 4, 2, 2) + piece, bf16),
            pltpu.VMEM((2, rows, kv), f32),
            pltpu.VMEM((2, rows, kv), f32),
            pltpu.VMEM((2, 2, rows, kv // 2), bf16),
            pltpu.VMEM((2, 2, rows, kv // 2), bf16),
            pltpu.VMEM((tok, 2 * kv), f32),
            pltpu.SemaphoreType.DMA((28,)),
            pltpu.SemaphoreType.DMA((COUNT,)),
            pltpu.SemaphoreType.DMA((COUNT,)),
        ],
        compiler_params=pltpu.CompilerParams(
            collective_id=0, has_side_effects=True, vmem_limit_bytes=62 * 2**20
        ),
        cost_estimate=pl.CostEstimate(
            flops=17_200_000_000, bytes_accessed=16 * 2**20, transcendentals=0
        ),
        name="outer_step",
    )(
        activations, cotangent, first_moment[0], second_moment[0], inner_params[0],
        global_params, outer_momentum,
    )
    new_first, new_second, new_momentum, new_global = pl.pallas_call(
        hand_over,
        out_shape=(state,) * 4,
        in_specs=[anywhere] * 4,
        out_specs=(anywhere,) * 4,
        scratch_shapes=[held] * 4 + [pltpu.SemaphoreType.DMA((8,))],
        cost_estimate=pl.CostEstimate(flops=0, bytes_accessed=4 * 2**20, transcendentals=0),
        name="hand_over",
    )(*states)
    return (
        new_first[None], new_second[None], new_momentum, new_global,
        projected.reshape(tok, 2, kv),
    )


def solution(mesh):
    in_specs = (
        P(("island", "fsdp"), "tensor"),
        P(("island", "fsdp"), None, "tensor"),
        P("island", "fsdp", None, "tensor"),
        P("island", "fsdp", None, "tensor"),
        P("island", "fsdp", None, "tensor"),
        P("fsdp", None, "tensor"),
        P("fsdp", None, "tensor"),
    )
    out_specs = (
        P("island", "fsdp", None, "tensor"),
        P("island", "fsdp", None, "tensor"),
        P("fsdp", None, "tensor"),
        P("fsdp", None, "tensor"),
        P(("island", "fsdp"), None, "tensor"),
    )
    return jax.shard_map(shards, mesh=mesh, in_specs=in_specs, out_specs=out_specs, check_vma=False)
```

```python
import functools

import jax
import jax.numpy as jnp
from jax import lax
from jax.experimental import pallas as pl
from jax.experimental.pallas import tpu as pltpu
from jax.sharding import PartitionSpec as P

D = 8192
STEP = 20
beta_one = 0.9
beta_two = 0.95
adam_eps = 1e-08
inner_rate = 0.05
weight_decay = 0.1
outer_rate = 0.7
outer_mu = 0.9

MESH = pl.DeviceIdType.MESH
bf16 = jnp.bfloat16
f32 = jnp.float32

ORDER = [
    (2, 2), (2, 1), (1, 2), (2, 3), (3, 2), (1, 1), (3, 3), (1, 3),
    (3, 1), (0, 2), (2, 0), (0, 1), (1, 0), (0, 3), (3, 0), (0, 0),
]
ARRIVAL = [
    (0, 0), (0, 1), (1, 0), (0, 3), (3, 0), (0, 2), (2, 0), (1, 1),
    (3, 3), (1, 3), (3, 1), (1, 2), (2, 1), (3, 2), (2, 3), (2, 2),
]


SCHEDULE = [
    ("G", 0), ("S", 0, 0), ("G", 1), ("S", 0, 1), ("G", 2), ("S", 0, 2), ("G", 3), ("S", 0, 3), ("G", 4),
    ("B", 0, 2, 1), ("S", 0, 4), ("Y", 0), ("S", 1, 0), ("G", 5), ("B", 0, 2, 0), ("G", 6), ("S", 0, 6),
    ("S", 0, 5), ("G", 7), ("G", 8), ("S", 0, 7), ("S", 0, 8), ("B", 0, 1, 0), ("B", 0, 3, 1), ("G", 9),
    ("S", 0, 9), ("B", 0, 1, 1), ("G", 10), ("C", 0, 2, 0), ("Y", 1), ("B", 0, 3, 0), ("G", 11), ("S", 1, 1),
    ("C", 0, 2, 1), ("S", 0, 10), ("G", 12), ("G", 13), ("G", 14), ("S", 0, 13), ("C", 0, 3, 0), ("S", 0, 14),
    ("C", 0, 1, 0), ("S", 0, 11), ("B", 0, 0, 0), ("T",), ("C", 0, 3, 1), ("C", 0, 1, 1), ("S", 0, 12),
    ("Y", 2), ("Y", 3), ("B", 1, 2, 0), ("Y", 5), ("B", 0, 0, 1), ("S", 1, 3), ("Y", 4), ("Y", 11),
    ("S", 1, 4), ("Y", 9), ("Y", 10), ("G", 15), ("S", 1, 2), ("Y", 6), ("B", 1, 2, 1), ("Y", 12),
    ("S", 1, 10), ("C", 0, 0, 0), ("E", 0, 0), ("Y", 8), ("Y", 7), ("S", 1, 5), ("C", 0, 0, 1), ("S", 1, 6),
    ("E", 0, 1), ("S", 1, 9), ("B", 1, 1, 1), ("Y", 13), ("Y", 14), ("S", 1, 8), ("S", 1, 7), ("B", 1, 3, 1),
    ("B", 1, 3, 0), ("C", 1, 2, 0), ("B", 1, 1, 0), ("S", 1, 13), ("S", 1, 11), ("A", 0, 0), ("A", 0, 1),
    ("C", 1, 2, 1), ("C", 1, 1, 1), ("S", 1, 12), ("B", 1, 0, 1), ("S", 1, 14), ("Y", 15), ("C", 1, 3, 1),
    ("B", 1, 0, 0), ("C", 1, 3, 0), ("C", 1, 1, 0), ("O", 0), ("C", 1, 0, 1), ("E", 1, 1), ("C", 1, 0, 0),
    ("E", 1, 0), ("Z", 0), ("K", 0, 0, 0), ("A", 1, 1), ("K", 0, 1, 0), ("A", 1, 0), ("I", 0, 1, 3),
    ("I", 0, 0, 1), ("I", 0, 1, 1), ("I", 0, 0, 3), ("I", 0, 0, 2), ("I", 0, 1, 2), ("O", 1), ("K", 0, 1, 1),
    ("M", 0, 1, 3), ("M", 0, 0, 1), ("K", 0, 0, 3), ("K", 0, 1, 2), ("N", 0, 1, 0), ("P", 0, 7),
    ("N", 0, 0, 0), ("P", 0, 0), ("Z", 1), ("P", 0, 1), ("K", 0, 0, 2), ("M", 0, 1, 1), ("P", 0, 5),
    ("K", 1, 0, 0), ("N", 0, 1, 1), ("M", 0, 0, 0), ("P", 0, 2), ("N", 0, 0, 3), ("K", 0, 1, 3),
    ("I", 1, 1, 3), ("M", 0, 0, 3), ("K", 1, 1, 0), ("I", 1, 0, 3), ("N", 0, 1, 2), ("K", 0, 0, 1),
    ("P", 0, 6), ("M", 0, 1, 0), ("P", 1, 0), ("M", 0, 1, 2), ("N", 0, 0, 2), ("P", 0, 8), ("N", 0, 1, 3),
    ("I", 1, 1, 1), ("I", 1, 0, 1), ("M", 1, 0, 0), ("N", 1, 0, 0), ("I", 1, 0, 2), ("P", 1, 2),
    ("K", 1, 1, 3), ("M", 0, 0, 2), ("I", 1, 1, 2), ("K", 1, 0, 3), ("M", 1, 1, 0), ("P", 0, 3),
    ("N", 1, 1, 0), ("P", 0, 10), ("N", 0, 0, 1), ("P", 0, 15), ("K", 1, 1, 1), ("M", 1, 0, 3),
    ("K", 1, 0, 1), ("M", 1, 1, 3), ("P", 1, 1), ("P", 0, 9), ("N", 1, 1, 3), ("P", 0, 4), ("P", 0, 12),
    ("K", 1, 0, 2), ("N", 1, 0, 3), ("M", 1, 0, 1), ("P", 0, 11), ("P", 0, 13), ("N", 1, 1, 1),
    ("N", 1, 0, 1), ("K", 1, 1, 2), ("P", 1, 4), ("M", 1, 1, 1), ("M", 1, 0, 2), ("P", 1, 5), ("M", 1, 1, 2),
    ("P", 1, 3), ("N", 1, 0, 2), ("P", 1, 11), ("P", 0, 14), ("P", 1, 7), ("N", 1, 1, 2), ("P", 1, 12),
    ("P", 1, 8), ("P", 1, 6), ("P", 1, 10), ("P", 1, 9), ("P", 1, 13), ("P", 1, 14), ("P", 1, 15),
]


class Numbers:
    def __init__(self):
        self.of = {}

    def __call__(self, key):
        return self.of.setdefault(key, len(self.of))


def kernel(
    count, x_hbm, c_hbm, m_hbm, v_hbm, th_hbm, gp_hbm, om_hbm,
    nf_hbm, ns_hbm, nm_hbm, ng_hbm, out_hbm,
    cot, ct, m_ref, v_ref, th_ref, gp_ref, om_ref, nf, ns, nm, ng, out,
    Xc, Pt, Fs, Fr, A2, Ap, Am, B2, Bp, Bm, Zs, Zr, F, W, Ts, Tr, As, Ar, acc,
    lsem, ssem, rsem,
):
    i = lax.axis_index("island")
    f = lax.axis_index("fsdp")
    t = lax.axis_index("tensor")
    hme = lax.rem(f, 2)
    oh = 1 - hme
    x = lax.rem(lax.div(f, 2), 4)
    y = lax.div(f, 8)

    def wrap(v):
        return lax.rem(v, 4)

    def dev(xx, yy, hh, ii, tt):
        return {"island": ii, "fsdp": (yy * 4 + xx) * 2 + hh, "tensor": tt}

    peer = dev(x, y, hme, i, 1 - t)
    zfar = dev(x, y, oh, i, t)
    zisl = dev(x, y, hme, 1 - i, t)
    zmir = dev(x, y, oh, 1 - i, t)

    sense = 1 + 2 * i

    def near(axis, s):
        if axis == 0:
            return dev(wrap(x + s), y, hme, i, t)
        return dev(x, wrap(y + s), hme, i, t)

    numbers = Numbers()
    sent = []
    waited = set()

    def message(key, src, dst, to):
        n = numbers(key)
        return pltpu.make_async_remote_copy(
            src_ref=src, dst_ref=dst, send_sem=ssem.at[n], recv_sem=rsem.at[n],
            device_id=to, device_id_type=MESH,
        )

    def send(key, src, dst, to):
        message(key, src, dst, to).start()
        sent.append((key, src, dst, to))

    def recv(key, dst):
        if key not in waited:
            waited.add(key)
            message(key, dst, dst, peer).wait_recv()

    barrier = pltpu.get_barrier_semaphore()
    friends = [near(a, g) for a in range(2) for g in (1, 2, 3)] + [peer, zfar, zisl, zmir]
    for d in friends:
        pl.semaphore_signal(barrier, inc=1, device_id=d, device_id_type=MESH)

    state_in = [
        pltpu.make_async_copy(a, b, lsem.at[16 + n])
        for n, (a, b) in enumerate((
            (c_hbm, cot), (th_hbm, th_ref), (gp_hbm, gp_ref),
            (m_hbm, m_ref), (v_hbm, v_ref), (om_hbm, om_ref),
        ))
    ]
    state_in[0].start()

    def place(p, ja, jb):
        dx, dy = (ja, jb) if p == 0 else (jb, ja)
        return wrap(y + dy), wrap(x + dx)

    def chunk(c):
        dy, dx = ORDER[c]
        yy, xx = wrap(y + dy), wrap(x + dx)
        k = yy * 4 + xx
        mine = lax.div(yy, 2) == t
        src = x_hbm.at[:, pl.ds(pl.multiple_of(lax.rem(k, 8) * 512, 512), 512)]
        return k, mine, src

    for c in range(16):
        k, mine, src = chunk(c)

        @pl.when(mine)
        def _():
            pltpu.make_async_copy(src, Xc.at[k], lsem.at[c]).start()

    for copy in state_in[1:]:
        copy.start()
    state_in[0].wait()
    for u in range(2):
        ct[u * 256 : (u + 1) * 256, :] = cot[:, u, :].T

    pl.semaphore_wait(barrier, len(friends))
    for c in range(16):
        k, mine, src = chunk(c)
        n = numbers(("X", c))

        @pl.when(mine)
        def _():
            message(("X", c), src, Xc.at[k], peer).start()

    def gradient(c):
        k, mine, src = chunk(c)

        @pl.when(mine)
        def _():
            pltpu.make_async_copy(src, Xc.at[k], lsem.at[c]).wait()

        @pl.when(jnp.logical_not(mine))
        def _():
            message(("X", c), Xc.at[k], Xc.at[k], peer).wait_recv()

        dy, dx = ORDER[c]
        yy, xx = wrap(y + dy), wrap(x + dx)
        for h in range(2):
            part = jnp.dot(
                ct[...], Xc[k, :, h * 256 : (h + 1) * 256], preferred_element_type=f32
            ).astype(bf16)
            for p in range(2):
                r = p * 128
                Pt[0, p, yy, xx, h] = part[r : r + 128]
                r = 256 + p * 128
                Pt[1, p, yy, xx, h, 0:64] = part[r : r + 64]
                Fs[yy, xx, h, p] = part[r + 64 : r + 128]
        send(("F", c), Fs.at[yy, xx, oh], Fr.at[yy, xx], zfar)

    def fold(c):
        dy, dx = ORDER[c]
        yy, xx = wrap(y + dy), wrap(x + dx)
        recv(("F", c), Fr.at[yy, xx])
        for p in range(2):
            total = (Fs[yy, xx, hme, p].astype(f32) + Fr[yy, xx, p].astype(f32)).astype(bf16)
            for h in range(2):
                Pt[1, p, yy, xx, h, 64:96] = total[32 * h : 32 * h + 32]

    def cut(u):
        return pl.ds(0, 128 if u == 0 else 96)

    def Pc(u, p, ja, jb, h):
        yy, xx = place(p, ja, jb)
        return Pt.at[u, p, yy, xx, h, cut(u)]

    def Pb(u, p, ja, jb):
        yy, xx = place(p, ja, jb)
        return Pt.at[u, p, yy, xx, :, cut(u)]

    def slot(ref, u, p, jb, h):
        return ref.at[u, p, jb, h, cut(u)]

    def first_sends(u, c):
        dy, dx = ORDER[c]
        for p in range(2):
            ja, jb = (dx, dy) if p == 0 else (dy, dx)
            if ja == 2:
                send(("A2", u, p, jb, 0), Pc(u, p, 2, jb, 0), slot(A2, u, p, jb, 0), near(p, 1))
                send(("A2", u, p, jb, 1), Pc(u, p, 2, jb, 1), slot(A2, u, p, jb, 1), near(p, 3))
            elif ja == 1:
                send(("Am", u, p, jb, 1), Pc(u, p, 1, jb, 1), slot(Am, u, p, jb, 1), near(p, 1))
            elif ja == 3:
                send(("Ap", u, p, jb, 0), Pc(u, p, 3, jb, 0), slot(Ap, u, p, jb, 0), near(p, 3))

    def add_to(dst, src):
        dst[...] = (dst[...].astype(f32) + src[...].astype(f32)).astype(bf16)

    def middle(u, jb, p):
        own, far = Pc(u, p, 1, jb, 0), slot(A2, u, p, jb, 0)
        recv(("A2", u, p, jb, 0), far)
        add_to(own, far)
        send(("Am", u, p, jb, 0), own, slot(Am, u, p, jb, 0), near(p, 1))
        own, far = Pc(u, p, 3, jb, 1), slot(A2, u, p, jb, 1)
        recv(("A2", u, p, jb, 1), far)
        add_to(own, far)
        send(("Ap", u, p, jb, 1), own, slot(Ap, u, p, jb, 1), near(p, 3))

    def close(u, jb, p):
        for h in range(2):
            below, above = slot(Am, u, p, jb, h), slot(Ap, u, p, jb, h)
            recv(("Am", u, p, jb, h), below)
            recv(("Ap", u, p, jb, h), above)
            own = Pc(u, p, 0, jb, h)
            total = own[...].astype(f32) + below[...].astype(f32) + above[...].astype(f32)
            if jb == 0:
                F[u, p, h, cut(u)] = total
            else:
                own[...] = total.astype(bf16)
        if jb != 0:
            name, ref = {1: ("Bm", Bm), 2: ("B2", B2), 3: ("Bp", Bp)}[jb]
            send((name, u, p), Pb(u, p, 0, jb), ref.at[u, p, :, cut(u)], near(1 - p, jb))

    def second(u, p):
        refs = [ref.at[u, p, :, cut(u)] for ref in (Bm, Bp, B2)]
        for name, ref in zip(("Bm", "Bp", "B2"), refs):
            recv((name, u, p), ref)
        for h in range(2):
            more = [ref[u, p, h, cut(u)].astype(f32) for ref in (Bm, Bp, B2)]
            F[u, p, h, cut(u)] = F[u, p, h, cut(u)] + (more[0] + more[1] + more[2])
        n = pl.ds(0, 128 if u == 0 else 64)
        Zs[u, p, n] = F[u, p, oh, n].astype(bf16)
        send(("Z", u, p), Zs.at[u, p, n], Zr.at[u, p, n], zfar)

    def start_islands():
        for copy in state_in[1:]:
            copy.wait()
        for u in range(2):
            th = th_ref[:, u, :]
            Ts[u] = gp_ref[:, u, :] - (th - (inner_rate * weight_decay) * th)
        send(("T",), Ts, Tr, zisl)

    def adam(u, p):
        cols = slice(p * 128, (p + 1) * 128)
        n = pl.ds(0, 128 if u == 0 else 64)
        recv(("Z", u, p), Zr.at[u, p, n])
        total = F[u, p, hme, n] + Zr[u, p, n].astype(f32)
        if u == 1:
            total = jnp.concatenate([total, F[u, p, 0, 64:96], F[u, p, 1, 64:96]], axis=0)
        grad = total.T
        first = beta_one * m_ref[:, u, cols] + (1.0 - beta_one) * grad
        second = beta_two * v_ref[:, u, cols] + (1.0 - beta_two) * grad * grad
        nf[:, u, cols] = first
        ns[:, u, cols] = second
        ascent = (
            first / (1.0 - beta_one**STEP)
            / (jnp.sqrt(second / (1.0 - beta_two**STEP)) + adam_eps)
        )
        As[u, p] = ascent.astype(bf16)
        send(("I", u, p), As.at[u, p], Ar.at[u, p], zisl)

    def place_w(p, ja, jb):
        return place(p, sense * ja, sense * jb)

    def near_w(axis, g):
        return near(axis, sense * g)

    def Wp(u, p, ja, jb):
        yy, xx = place_w(p, ja, jb)
        return W.at[u, yy, xx, :, p]

    def Wh(u, p, ja, jb, h):
        yy, xx = place_w(p, ja, jb)
        return W.at[u, yy, xx, h, p]

    def outer(u):
        recv(("T",), Tr)
        for p in range(2):
            cols = slice(p * 128, (p + 1) * 128)
            recv(("I", u, p), Ar.at[u, p])
            steps = As[u, p].astype(f32) + Ar[u, p].astype(f32)
            delta = ((Ts[u, :, cols] + Tr[u, :, cols]) + inner_rate * steps) * 0.5
            momentum = outer_mu * om_ref[:, u, cols] + delta
            fresh = gp_ref[:, u, cols] - outer_rate * (delta + outer_mu * momentum)
            nm[:, u, cols] = momentum
            ng[:, u, cols] = fresh
            low = fresh.astype(bf16)
            W[u, y, x, hme, 0, :, cols] = low[:128]
            W[u, y, x, hme, 1, :, cols] = low[128:]
        send(("Gz", u), W.at[u, y, x, hme], W.at[u, y, x, hme], zmir)
        spread(u, 0)

    def spread(u, s):
        h = hme if s == 0 else oh
        for p in range(2):
            ref = Wh(u, p, 0, 0, h)
            for g in (1, 3, 2):
                send(("G1", u, p, s, g), ref, ref, near_w(p, g))
            send(("G2b", u, p, 0, s), ref, ref, near_w(1 - p, 3))

            @pl.when(h == i)
            def _():
                message(("G2e", u, p, 0), ref, ref, near_w(1 - p, 1)).start()

            if s == 1:
                own = Wh(u, p, 0, 0, i)
                sent.append((("G2e", u, p, 0), own, own, near_w(1 - p, 1)))

    def agz(u):
        recv(("Gz", u), W.at[u, y, x, oh])
        spread(u, 1)

    def g2(u, p, j):
        ref = Wh(u, p, j, 0, i)
        send(("G2e", u, p, j), ref, ref, near_w(1 - p, 1))
        ref = Wp(u, p, j, 0)
        send(("G2b", u, p, j), ref, ref, near_w(1 - p, 3))

    def pass_on(u, p, j):
        recv(("G1", u, p, 0, 4 - j), Wh(u, p, j, 0, hme))
        recv(("G1", u, p, 1, 4 - j), Wh(u, p, j, 0, oh))
        g2(u, p, j)

    def ahead(u, p, j):
        if j == 0:
            recv(("G2b", u, p, 0, 0), Wh(u, p, 0, 1, hme))
            recv(("G2b", u, p, 0, 1), Wh(u, p, 0, 1, oh))
        else:
            recv(("G2b", u, p, j), Wp(u, p, j, 1))

    def onward(u, p, j):
        ref = Wh(u, p, j, 3, i)
        recv(("G2e", u, p, j), ref)
        send(("G2f", u, p, j), ref, ref, near_w(1 - p, 1))

    def to_mirror(u, p, j):
        ahead(u, p, j)
        ref = Wh(u, p, j, 1, i)
        send(("G2m", u, p, (4 - j) % 4), ref, ref, zmir)

    def to_island(u, p, j):
        ref = Wh(u, p, j, 2, i)
        recv(("G2f", u, p, j), ref)
        send(("G2z", u, p, (4 - j) % 4), ref, ref, zisl)

    leaving = []

    def leave(n, src, dst):
        copy = pltpu.make_async_copy(src, dst, lsem.at[22 + n])
        copy.start()
        leaving.append(copy)

    seen = {0: 0, 1: 0}

    def project(u, c):
        dy, dx = ARRIVAL[c]
        for p in range(2):
            ja, jb = (dx, dy) if p == 0 else (dy, dx)
            if jb == 1:
                ahead(u, p, ja)
            if jb == 3:
                recv(("G2e", u, p, ja), Wh(u, p, ja, 3, i))
                recv(("G2m", u, p, ja), Wh(u, p, ja, 3, 1 - i))
            if jb == 2:
                recv(("G2f", u, p, ja), Wh(u, p, ja, 2, i))
                recv(("G2z", u, p, ja), Wh(u, p, ja, 2, 1 - i))
        yy, xx = wrap(y + sense * dy), wrap(x + sense * dx)
        right = W[u, yy, xx].reshape(512, 256)
        part = jnp.dot(Xc[yy * 4 + xx], right, preferred_element_type=f32)
        cols = slice(u * 256, (u + 1) * 256)
        seen[u] += 1
        if seen[u] == 1:
            acc[:, cols] = part
        elif seen[u] < 16:
            acc[:, cols] += part
        else:
            out[:, cols] = ((acc[:, cols] + part) * D ** (-0.5)).astype(bf16)
            leave(4 + u, out.at[:, cols], out_hbm.at[:, cols])

    steps = {
        "G": gradient, "Y": fold, "T": start_islands, "S": first_sends, "B": middle, "C": close,
        "E": second, "A": adam, "O": outer, "Z": agz, "I": pass_on, "K": onward,
        "M": to_mirror, "N": to_island, "P": project,
    }
    counts = {}
    for name, *where in SCHEDULE:
        steps[name](*where)
        counts[name] = counts.get(name, 0) + 1
        if name == "A" and counts[name] == 4:
            leave(0, nf, nf_hbm)
            leave(1, ns, ns_hbm)
        if name == "O" and counts[name] == 2:
            leave(2, nm, nm_hbm)
            leave(3, ng, ng_hbm)

    for copy in leaving:
        copy.wait()
    for key, src, dst, to in sent:
        message(key, src, dst, to).wait_send()
    for c in range(16):
        k, mine, src = chunk(c)

        @pl.when(mine)
        def _():
            message(("X", c), src, Xc.at[k], peer).wait_send()

    if len(numbers.of) != count:
        raise ValueError(len(numbers.of))


COUNT = 259


def hand_over(*refs):
    ins, outs, held, sem = refs[:4], refs[4:8], refs[8:12], refs[12]
    there = [pltpu.make_async_copy(a, b, sem.at[n]) for n, (a, b) in enumerate(zip(ins, held))]
    back = [pltpu.make_async_copy(a, b, sem.at[4 + n]) for n, (a, b) in enumerate(zip(held, outs))]
    for copy in there:
        copy.start()
    for first, second in zip(there, back):
        first.wait()
        second.start()
    for copy in back:
        copy.wait()


def shards(
    activations, cotangent, inner_params, first_moment, second_moment, global_params, outer_momentum
):
    tok, kv = cotangent.shape[0], cotangent.shape[2]
    rows = global_params.shape[0]
    anywhere = pl.BlockSpec(memory_space=pl.ANY)
    state = jax.ShapeDtypeStruct((rows, 2, kv), f32)
    piece = (128, 256)
    held = pltpu.VMEM((rows, 2, kv), f32)
    *states, projected = pl.pallas_call(
        functools.partial(kernel, COUNT),
        out_shape=(state, state, state, state, jax.ShapeDtypeStruct((tok, 2 * kv), bf16)),
        in_specs=[anywhere] * 7,
        out_specs=(anywhere,) * 5,
        scratch_shapes=[
            pltpu.VMEM((tok, 2, kv), bf16),
            pltpu.VMEM((2 * kv, tok), bf16),
            held, held, held, held, held, held, held, held, held,
            pltpu.VMEM((tok, 2 * kv), bf16),
            pltpu.VMEM((16, tok, 512), bf16),
            pltpu.VMEM((2, 2, 4, 4, 2) + piece, bf16),
            pltpu.VMEM((4, 4, 2, 2, 64, 256), bf16),
            pltpu.VMEM((4, 4, 2, 64, 256), bf16),
            pltpu.VMEM((2, 2, 4, 2) + piece, bf16),
            pltpu.VMEM((2, 2, 4, 2) + piece, bf16),
            pltpu.VMEM((2, 2, 4, 2) + piece, bf16),
            pltpu.VMEM((2, 2, 2) + piece, bf16),
            pltpu.VMEM((2, 2, 2) + piece, bf16),
            pltpu.VMEM((2, 2, 2) + piece, bf16),
            pltpu.VMEM((2, 2) + piece, bf16),
            pltpu.VMEM((2, 2) + piece, bf16),
            pltpu.VMEM((2, 2, 2) + piece, f32),
            pltpu.VMEM((2, 4, 4, 2, 2) + piece, bf16),
            pltpu.VMEM((2, rows, kv), f32),
            pltpu.VMEM((2, rows, kv), f32),
            pltpu.VMEM((2, 2, rows, kv // 2), bf16),
            pltpu.VMEM((2, 2, rows, kv // 2), bf16),
            pltpu.VMEM((tok, 2 * kv), f32),
            pltpu.SemaphoreType.DMA((28,)),
            pltpu.SemaphoreType.DMA((COUNT,)),
            pltpu.SemaphoreType.DMA((COUNT,)),
        ],
        compiler_params=pltpu.CompilerParams(
            collective_id=0, has_side_effects=True, vmem_limit_bytes=62 * 2**20
        ),
        cost_estimate=pl.CostEstimate(
            flops=17_200_000_000, bytes_accessed=16 * 2**20, transcendentals=0
        ),
        name="outer_step",
    )(
        activations, cotangent, first_moment[0], second_moment[0], inner_params[0],
        global_params, outer_momentum,
    )
    new_first, new_second, new_momentum, new_global = pl.pallas_call(
        hand_over,
        out_shape=(state,) * 4,
        in_specs=[anywhere] * 4,
        out_specs=(anywhere,) * 4,
        scratch_shapes=[held] * 4 + [pltpu.SemaphoreType.DMA((8,))],
        cost_estimate=pl.CostEstimate(flops=0, bytes_accessed=4 * 2**20, transcendentals=0),
        name="hand_over",
    )(*states)
    return (
        new_first[None], new_second[None], new_momentum, new_global,
        projected.reshape(tok, 2, kv),
    )


def solution(mesh):
    in_specs = (
        P(("island", "fsdp"), "tensor"),
        P(("island", "fsdp"), None, "tensor"),
        P("island", "fsdp", None, "tensor"),
        P("island", "fsdp", None, "tensor"),
        P("island", "fsdp", None, "tensor"),
        P("fsdp", None, "tensor"),
        P("fsdp", None, "tensor"),
    )
    out_specs = (
        P("island", "fsdp", None, "tensor"),
        P("island", "fsdp", None, "tensor"),
        P("fsdp", None, "tensor"),
        P("fsdp", None, "tensor"),
        P(("island", "fsdp"), None, "tensor"),
    )
    return jax.shard_map(shards, mesh=mesh, in_specs=in_specs, out_specs=out_specs, check_vma=False)
```

```python
import functools

import jax
import jax.numpy as jnp
from jax import lax
from jax.experimental import pallas as pl
from jax.experimental.pallas import tpu as pltpu
from jax.sharding import PartitionSpec as P

D = 8192
STEP = 20
beta_one = 0.9
beta_two = 0.95
adam_eps = 1e-08
inner_rate = 0.05
weight_decay = 0.1
outer_rate = 0.7
outer_mu = 0.9

MESH = pl.DeviceIdType.MESH
bf16 = jnp.bfloat16
f32 = jnp.float32

ORDER = [
    (2, 2), (2, 1), (1, 2), (2, 3), (3, 2), (1, 1), (3, 3), (1, 3),
    (3, 1), (0, 2), (2, 0), (0, 1), (1, 0), (0, 3), (3, 0), (0, 0),
]
ARRIVAL = [
    (0, 0), (0, 1), (1, 0), (0, 3), (3, 0), (0, 2), (2, 0), (1, 1),
    (3, 3), (1, 3), (3, 1), (1, 2), (2, 1), (3, 2), (2, 3), (2, 2),
]


SCHEDULE = [
    ("G", 0), ("S", 0, 0), ("G", 1), ("S", 0, 1), ("G", 2), ("S", 0, 2), ("G", 3), ("S", 0, 3), ("G", 4),
    ("B", 0, 2, 1), ("S", 0, 4), ("Y", 0), ("S", 1, 0), ("G", 5), ("B", 0, 2, 0), ("G", 6), ("S", 0, 6),
    ("S", 0, 5), ("G", 7), ("G", 8), ("S", 0, 7), ("S", 0, 8), ("B", 0, 1, 0), ("B", 0, 3, 1), ("G", 9),
    ("S", 0, 9), ("B", 0, 1, 1), ("G", 10), ("C", 0, 2, 0), ("Y", 1), ("B", 0, 3, 0), ("G", 11), ("S", 1, 1),
    ("C", 0, 2, 1), ("S", 0, 10), ("R",), ("G", 12), ("G", 13), ("G", 14), ("S", 0, 13), ("C", 0, 3, 0), ("S", 0, 14),
    ("C", 0, 1, 0), ("S", 0, 11), ("B", 0, 0, 0), ("T",), ("C", 0, 3, 1), ("C", 0, 1, 1), ("S", 0, 12),
    ("Y", 2), ("Y", 3), ("B", 1, 2, 0), ("Y", 5), ("B", 0, 0, 1), ("S", 1, 3), ("Y", 4), ("Y", 11),
    ("S", 1, 4), ("Y", 9), ("Y", 10), ("G", 15), ("S", 1, 2), ("Y", 6), ("B", 1, 2, 1), ("Y", 12),
    ("S", 1, 10), ("C", 0, 0, 0), ("E", 0, 0), ("Y", 8), ("Y", 7), ("S", 1, 5), ("C", 0, 0, 1), ("S", 1, 6),
    ("E", 0, 1), ("S", 1, 9), ("B", 1, 1, 1), ("Y", 13), ("Y", 14), ("S", 1, 8), ("S", 1, 7), ("B", 1, 3, 1),
    ("B", 1, 3, 0), ("C", 1, 2, 0), ("B", 1, 1, 0), ("S", 1, 13), ("S", 1, 11), ("A", 0, 0), ("A", 0, 1),
    ("C", 1, 2, 1), ("C", 1, 1, 1), ("S", 1, 12), ("B", 1, 0, 1), ("S", 1, 14), ("Y", 15), ("C", 1, 3, 1),
    ("B", 1, 0, 0), ("C", 1, 3, 0), ("C", 1, 1, 0), ("O", 0), ("C", 1, 0, 1), ("E", 1, 1), ("C", 1, 0, 0),
    ("E", 1, 0), ("Z", 0), ("K", 0, 0, 0), ("A", 1, 1), ("K", 0, 1, 0), ("A", 1, 0), ("I", 0, 1, 3),
    ("I", 0, 0, 1), ("I", 0, 1, 1), ("I", 0, 0, 3), ("I", 0, 0, 2), ("I", 0, 1, 2), ("O", 1), ("K", 0, 1, 1),
    ("M", 0, 1, 3), ("M", 0, 0, 1), ("K", 0, 0, 3), ("K", 0, 1, 2), ("N", 0, 1, 0), ("P", 0, 7),
    ("N", 0, 0, 0), ("P", 0, 0), ("Z", 1), ("P", 0, 1), ("K", 0, 0, 2), ("M", 0, 1, 1), ("P", 0, 5),
    ("K", 1, 0, 0), ("N", 0, 1, 1), ("M", 0, 0, 0), ("P", 0, 2), ("N", 0, 0, 3), ("K", 0, 1, 3),
    ("I", 1, 1, 3), ("M", 0, 0, 3), ("K", 1, 1, 0), ("I", 1, 0, 3), ("N", 0, 1, 2), ("K", 0, 0, 1),
    ("P", 0, 6), ("M", 0, 1, 0), ("P", 1, 0), ("M", 0, 1, 2), ("N", 0, 0, 2), ("P", 0, 8), ("N", 0, 1, 3),
    ("I", 1, 1, 1), ("I", 1, 0, 1), ("M", 1, 0, 0), ("N", 1, 0, 0), ("I", 1, 0, 2), ("P", 1, 2),
    ("K", 1, 1, 3), ("M", 0, 0, 2), ("I", 1, 1, 2), ("K", 1, 0, 3), ("M", 1, 1, 0), ("P", 0, 3),
    ("N", 1, 1, 0), ("P", 0, 10), ("N", 0, 0, 1), ("P", 0, 15), ("K", 1, 1, 1), ("M", 1, 0, 3),
    ("K", 1, 0, 1), ("M", 1, 1, 3), ("P", 1, 1), ("P", 0, 9), ("N", 1, 1, 3), ("P", 0, 4), ("P", 0, 12),
    ("K", 1, 0, 2), ("N", 1, 0, 3), ("M", 1, 0, 1), ("P", 0, 11), ("P", 0, 13), ("N", 1, 1, 1),
    ("N", 1, 0, 1), ("K", 1, 1, 2), ("P", 1, 4), ("M", 1, 1, 1), ("M", 1, 0, 2), ("P", 1, 5), ("M", 1, 1, 2),
    ("P", 1, 3), ("N", 1, 0, 2), ("P", 1, 11), ("P", 0, 14), ("P", 1, 7), ("N", 1, 1, 2), ("P", 1, 12),
    ("P", 1, 8), ("P", 1, 6), ("P", 1, 10), ("P", 1, 9), ("P", 1, 13), ("P", 1, 14), ("P", 1, 15),
]


class Numbers:
    def __init__(self):
        self.of = {}

    def __call__(self, key):
        return self.of.setdefault(key, len(self.of))


def kernel(
    count, x_hbm, c_hbm, m_hbm, v_hbm, th_hbm, gp_hbm, om_hbm,
    nf_hbm, ns_hbm, nm_hbm, ng_hbm, out_hbm,
    cot, ct, m_ref, v_ref, th_ref, gp_ref, om_ref, nf, ns, nm, ng, out,
    Xc, Pt, Fs, Fr, A2, Ap, Am, B2, Bp, Bm, Zs, Zr, F, W, Ts, Tr, As, Ar, acc, Ms, Vs, Gs, Os,
    lsem, ssem, rsem,
):
    i = lax.axis_index("island")
    f = lax.axis_index("fsdp")
    t = lax.axis_index("tensor")
    hme = lax.rem(f, 2)
    oh = 1 - hme
    x = lax.rem(lax.div(f, 2), 4)
    y = lax.div(f, 8)

    def wrap(v):
        return lax.rem(v, 4)

    def dev(xx, yy, hh, ii, tt):
        return {"island": ii, "fsdp": (yy * 4 + xx) * 2 + hh, "tensor": tt}

    peer = dev(x, y, hme, i, 1 - t)
    zfar = dev(x, y, oh, i, t)
    zisl = dev(x, y, hme, 1 - i, t)
    zmir = dev(x, y, oh, 1 - i, t)

    sense = 1 + 2 * i

    def near(axis, s):
        if axis == 0:
            return dev(wrap(x + s), y, hme, i, t)
        return dev(x, wrap(y + s), hme, i, t)

    numbers = Numbers()
    sent = []
    waited = set()

    def message(key, src, dst, to):
        n = numbers(key)
        return pltpu.make_async_remote_copy(
            src_ref=src, dst_ref=dst, send_sem=ssem.at[n], recv_sem=rsem.at[n],
            device_id=to, device_id_type=MESH,
        )

    def send(key, src, dst, to):
        message(key, src, dst, to).start()
        sent.append((key, src, dst, to))

    def recv(key, dst):
        if key not in waited:
            waited.add(key)
            message(key, dst, dst, peer).wait_recv()

    barrier = pltpu.get_barrier_semaphore()
    friends = [near(a, g) for a in range(2) for g in (1, 2, 3)] + [peer, zfar, zisl, zmir]
    for d in friends:
        pl.semaphore_signal(barrier, inc=1, device_id=d, device_id_type=MESH)

    state_in = [
        pltpu.make_async_copy(a, b, lsem.at[16 + n])
        for n, (a, b) in enumerate((
            (c_hbm, cot), (th_hbm, th_ref), (gp_hbm, gp_ref),
            (m_hbm, m_ref), (v_hbm, v_ref), (om_hbm, om_ref),
        ))
    ]
    state_in[0].start()

    def place(p, ja, jb):
        dx, dy = (ja, jb) if p == 0 else (jb, ja)
        return wrap(y + dy), wrap(x + dx)

    def chunk(c):
        dy, dx = ORDER[c]
        yy, xx = wrap(y + dy), wrap(x + dx)
        k = yy * 4 + xx
        mine = lax.div(yy, 2) == t
        src = x_hbm.at[:, pl.ds(pl.multiple_of(lax.rem(k, 8) * 512, 512), 512)]
        return k, mine, src

    for c in range(16):
        k, mine, src = chunk(c)

        @pl.when(mine)
        def _():
            pltpu.make_async_copy(src, Xc.at[k], lsem.at[c]).start()

    for copy in state_in[1:]:
        copy.start()
    pl.semaphore_wait(barrier, len(friends))
    for c in range(16):
        k, mine, src = chunk(c)
        n = numbers(("X", c))

        @pl.when(mine)
        def _():
            message(("X", c), src, Xc.at[k], peer).start()

    state_in[0].wait()
    for u in range(2):
        ct[u * 256 : (u + 1) * 256, :] = cot[:, u, :].T

    def gradient(c):
        k, mine, src = chunk(c)

        @pl.when(mine)
        def _():
            pltpu.make_async_copy(src, Xc.at[k], lsem.at[c]).wait()

        @pl.when(jnp.logical_not(mine))
        def _():
            message(("X", c), Xc.at[k], Xc.at[k], peer).wait_recv()

        dy, dx = ORDER[c]
        yy, xx = wrap(y + dy), wrap(x + dx)
        for h in range(2):
            part = jnp.dot(
                ct[...], Xc[k, :, h * 256 : (h + 1) * 256], preferred_element_type=f32
            ).astype(bf16)
            for p in range(2):
                r = p * 128
                Pt[0, p, yy, xx, h] = part[r : r + 128]
                r = 256 + p * 128
                Pt[1, p, yy, xx, h, 0:64] = part[r : r + 64]
                Fs[yy, xx, h, p] = part[r + 64 : r + 128]
        send(("F", c), Fs.at[yy, xx, oh], Fr.at[yy, xx], zfar)

    def fold(c):
        dy, dx = ORDER[c]
        yy, xx = wrap(y + dy), wrap(x + dx)
        recv(("F", c), Fr.at[yy, xx])
        for p in range(2):
            total = (Fs[yy, xx, hme, p].astype(f32) + Fr[yy, xx, p].astype(f32)).astype(bf16)
            for h in range(2):
                Pt[1, p, yy, xx, h, 64:96] = total[32 * h : 32 * h + 32]

    def cut(u):
        return pl.ds(0, 128 if u == 0 else 96)

    def Pc(u, p, ja, jb, h):
        yy, xx = place(p, ja, jb)
        return Pt.at[u, p, yy, xx, h, cut(u)]

    def Pb(u, p, ja, jb):
        yy, xx = place(p, ja, jb)
        return Pt.at[u, p, yy, xx, :, cut(u)]

    def slot(ref, u, p, jb, h):
        return ref.at[u, p, jb, h, cut(u)]

    def first_sends(u, c):
        dy, dx = ORDER[c]
        for p in range(2):
            ja, jb = (dx, dy) if p == 0 else (dy, dx)
            if ja == 2:
                send(("A2", u, p, jb, 0), Pc(u, p, 2, jb, 0), slot(A2, u, p, jb, 0), near(p, 1))
                send(("A2", u, p, jb, 1), Pc(u, p, 2, jb, 1), slot(A2, u, p, jb, 1), near(p, 3))
            elif ja == 1:
                send(("Am", u, p, jb, 1), Pc(u, p, 1, jb, 1), slot(Am, u, p, jb, 1), near(p, 1))
            elif ja == 3:
                send(("Ap", u, p, jb, 0), Pc(u, p, 3, jb, 0), slot(Ap, u, p, jb, 0), near(p, 3))

    def add_to(dst, src):
        dst[...] = (dst[...].astype(f32) + src[...].astype(f32)).astype(bf16)

    def middle(u, jb, p):
        own, far = Pc(u, p, 1, jb, 0), slot(A2, u, p, jb, 0)
        recv(("A2", u, p, jb, 0), far)
        add_to(own, far)
        send(("Am", u, p, jb, 0), own, slot(Am, u, p, jb, 0), near(p, 1))
        own, far = Pc(u, p, 3, jb, 1), slot(A2, u, p, jb, 1)
        recv(("A2", u, p, jb, 1), far)
        add_to(own, far)
        send(("Ap", u, p, jb, 1), own, slot(Ap, u, p, jb, 1), near(p, 3))

    def close(u, jb, p):
        for h in range(2):
            below, above = slot(Am, u, p, jb, h), slot(Ap, u, p, jb, h)
            recv(("Am", u, p, jb, h), below)
            recv(("Ap", u, p, jb, h), above)
            own = Pc(u, p, 0, jb, h)
            total = own[...].astype(f32) + below[...].astype(f32) + above[...].astype(f32)
            if jb == 0:
                F[u, p, h, cut(u)] = total
            else:
                own[...] = total.astype(bf16)
        if jb != 0:
            name, ref = {1: ("Bm", Bm), 2: ("B2", B2), 3: ("Bp", Bp)}[jb]
            send((name, u, p), Pb(u, p, 0, jb), ref.at[u, p, :, cut(u)], near(1 - p, jb))

    def second(u, p):
        refs = [ref.at[u, p, :, cut(u)] for ref in (Bm, Bp, B2)]
        for name, ref in zip(("Bm", "Bp", "B2"), refs):
            recv((name, u, p), ref)
        for h in range(2):
            more = [ref[u, p, h, cut(u)].astype(f32) for ref in (Bm, Bp, B2)]
            F[u, p, h, cut(u)] = F[u, p, h, cut(u)] + (more[0] + more[1] + more[2])
        n = pl.ds(0, 128 if u == 0 else 64)
        Zs[u, p, n] = F[u, p, oh, n].astype(bf16)
        send(("Z", u, p), Zs.at[u, p, n], Zr.at[u, p, n], zfar)

    def start_islands():
        state_in[1].wait()
        for u in range(2):
            th = th_ref[:, u, :]
            Ts[u] = gp_ref[:, u, :] - (th - (inner_rate * weight_decay) * th)
        send(("T",), Ts, Tr, zisl)

    def plain_states():
        for copy in state_in[2:]:
            copy.wait()
        for u in range(2):
            for flat, ref in ((Ms, m_ref), (Vs, v_ref), (Gs, gp_ref), (Os, om_ref)):
                flat[u] = ref[:, u, :]

    def adam(u, p):
        cols = slice(p * 128, (p + 1) * 128)
        n = pl.ds(0, 128 if u == 0 else 64)
        recv(("Z", u, p), Zr.at[u, p, n])
        total = F[u, p, hme, n] + Zr[u, p, n].astype(f32)
        if u == 1:
            total = jnp.concatenate([total, F[u, p, 0, 64:96], F[u, p, 1, 64:96]], axis=0)
        grad = total.T
        first = beta_one * Ms[u, :, cols] + (1.0 - beta_one) * grad
        second = beta_two * Vs[u, :, cols] + (1.0 - beta_two) * grad * grad
        ascent = (
            first / (1.0 - beta_one**STEP)
            / (jnp.sqrt(second / (1.0 - beta_two**STEP)) + adam_eps)
        )
        As[u, p] = ascent.astype(bf16)
        send(("I", u, p), As.at[u, p], Ar.at[u, p], zisl)
        nf[:, u, cols] = first
        ns[:, u, cols] = second

    def place_w(p, ja, jb):
        return place(p, sense * ja, sense * jb)

    def near_w(axis, g):
        return near(axis, sense * g)

    def Wp(u, p, ja, jb):
        yy, xx = place_w(p, ja, jb)
        return W.at[u, yy, xx, :, p]

    def Wh(u, p, ja, jb, h):
        yy, xx = place_w(p, ja, jb)
        return W.at[u, yy, xx, h, p]

    def outer(u):
        recv(("T",), Tr)
        results = []
        for p in range(2):
            cols = slice(p * 128, (p + 1) * 128)
            recv(("I", u, p), Ar.at[u, p])
            steps = As[u, p].astype(f32) + Ar[u, p].astype(f32)
            delta = ((Ts[u, :, cols] + Tr[u, :, cols]) + inner_rate * steps) * 0.5
            momentum = outer_mu * Os[u, :, cols] + delta
            fresh = Gs[u, :, cols] - outer_rate * (delta + outer_mu * momentum)
            results.append((cols, momentum, fresh))
            low = fresh.astype(bf16)
            W[u, y, x, hme, 0, :, cols] = low[:128]
            W[u, y, x, hme, 1, :, cols] = low[128:]
        send(("Gz", u), W.at[u, y, x, hme], W.at[u, y, x, hme], zmir)
        spread(u, 0)
        for cols, momentum, fresh in results:
            nm[:, u, cols] = momentum
            ng[:, u, cols] = fresh

    def spread(u, s):
        h = hme if s == 0 else oh
        for p in range(2):
            ref = Wh(u, p, 0, 0, h)
            for g in (1, 3, 2):
                send(("G1", u, p, s, g), ref, ref, near_w(p, g))
            send(("G2b", u, p, 0, s), ref, ref, near_w(1 - p, 3))

            @pl.when(h == i)
            def _():
                message(("G2e", u, p, 0), ref, ref, near_w(1 - p, 1)).start()

            if s == 1:
                own = Wh(u, p, 0, 0, i)
                sent.append((("G2e", u, p, 0), own, own, near_w(1 - p, 1)))

    def agz(u):
        recv(("Gz", u), W.at[u, y, x, oh])
        spread(u, 1)

    def g2(u, p, j):
        ref = Wh(u, p, j, 0, i)
        send(("G2e", u, p, j), ref, ref, near_w(1 - p, 1))
        ref = Wp(u, p, j, 0)
        send(("G2b", u, p, j), ref, ref, near_w(1 - p, 3))

    def pass_on(u, p, j):
        recv(("G1", u, p, 0, 4 - j), Wh(u, p, j, 0, hme))
        recv(("G1", u, p, 1, 4 - j), Wh(u, p, j, 0, oh))
        g2(u, p, j)

    def ahead(u, p, j):
        if j == 0:
            recv(("G2b", u, p, 0, 0), Wh(u, p, 0, 1, hme))
            recv(("G2b", u, p, 0, 1), Wh(u, p, 0, 1, oh))
        else:
            recv(("G2b", u, p, j), Wp(u, p, j, 1))

    def onward(u, p, j):
        ref = Wh(u, p, j, 3, i)
        recv(("G2e", u, p, j), ref)
        send(("G2f", u, p, j), ref, ref, near_w(1 - p, 1))

    def to_mirror(u, p, j):
        ahead(u, p, j)
        ref = Wh(u, p, j, 1, i)
        send(("G2m", u, p, (4 - j) % 4), ref, ref, zmir)

    def to_island(u, p, j):
        ref = Wh(u, p, j, 2, i)
        recv(("G2f", u, p, j), ref)
        send(("G2z", u, p, (4 - j) % 4), ref, ref, zisl)

    leaving = []

    def leave(n, src, dst):
        copy = pltpu.make_async_copy(src, dst, lsem.at[22 + n])
        copy.start()
        leaving.append(copy)

    seen = {0: 0, 1: 0}

    def project(u, c):
        dy, dx = ARRIVAL[c]
        for p in range(2):
            ja, jb = (dx, dy) if p == 0 else (dy, dx)
            if jb == 1:
                ahead(u, p, ja)
            if jb == 3:
                recv(("G2e", u, p, ja), Wh(u, p, ja, 3, i))
                recv(("G2m", u, p, ja), Wh(u, p, ja, 3, 1 - i))
            if jb == 2:
                recv(("G2f", u, p, ja), Wh(u, p, ja, 2, i))
                recv(("G2z", u, p, ja), Wh(u, p, ja, 2, 1 - i))
        yy, xx = wrap(y + sense * dy), wrap(x + sense * dx)
        right = W[u, yy, xx].reshape(512, 256)
        part = jnp.dot(Xc[yy * 4 + xx], right, preferred_element_type=f32)
        cols = slice(u * 256, (u + 1) * 256)
        seen[u] += 1
        if seen[u] == 1:
            acc[:, cols] = part
        elif seen[u] < 16:
            acc[:, cols] += part
        else:
            out[:, cols] = ((acc[:, cols] + part) * D ** (-0.5)).astype(bf16)
            leave(4 + u, out.at[:, cols], out_hbm.at[:, cols])

    steps = {
        "G": gradient, "Y": fold, "T": start_islands, "R": plain_states, "S": first_sends, "B": middle, "C": close,
        "E": second, "A": adam, "O": outer, "Z": agz, "I": pass_on, "K": onward,
        "M": to_mirror, "N": to_island, "P": project,
    }
    counts = {}
    for name, *where in SCHEDULE:
        steps[name](*where)
        counts[name] = counts.get(name, 0) + 1
        if name == "A" and counts[name] == 4:
            leave(0, nf, nf_hbm)
            leave(1, ns, ns_hbm)
        if name == "O" and counts[name] == 2:
            leave(2, nm, nm_hbm)
            leave(3, ng, ng_hbm)

    for copy in leaving:
        copy.wait()
    for key, src, dst, to in sent:
        message(key, src, dst, to).wait_send()
    for c in range(16):
        k, mine, src = chunk(c)

        @pl.when(mine)
        def _():
            message(("X", c), src, Xc.at[k], peer).wait_send()

    if len(numbers.of) != count:
        raise ValueError(len(numbers.of))


COUNT = 259


def hand_over(*refs):
    ins, outs, held, sem = refs[:4], refs[4:8], refs[8:12], refs[12]
    there = [pltpu.make_async_copy(a, b, sem.at[n]) for n, (a, b) in enumerate(zip(ins, held))]
    back = [pltpu.make_async_copy(a, b, sem.at[4 + n]) for n, (a, b) in enumerate(zip(held, outs))]
    for copy in there:
        copy.start()
    for first, second in zip(there, back):
        first.wait()
        second.start()
    for copy in back:
        copy.wait()


def shards(
    activations, cotangent, inner_params, first_moment, second_moment, global_params, outer_momentum
):
    tok, kv = cotangent.shape[0], cotangent.shape[2]
    rows = global_params.shape[0]
    anywhere = pl.BlockSpec(memory_space=pl.ANY)
    state = jax.ShapeDtypeStruct((rows, 2, kv), f32)
    piece = (128, 256)
    held = pltpu.VMEM((rows, 2, kv), f32)
    *states, projected = pl.pallas_call(
        functools.partial(kernel, COUNT),
        out_shape=(state, state, state, state, jax.ShapeDtypeStruct((tok, 2 * kv), bf16)),
        in_specs=[anywhere] * 7,
        out_specs=(anywhere,) * 5,
        scratch_shapes=[
            pltpu.VMEM((tok, 2, kv), bf16),
            pltpu.VMEM((2 * kv, tok), bf16),
            held, held, held, held, held, held, held, held, held,
            pltpu.VMEM((tok, 2 * kv), bf16),
            pltpu.VMEM((16, tok, 512), bf16),
            pltpu.VMEM((2, 2, 4, 4, 2) + piece, bf16),
            pltpu.VMEM((4, 4, 2, 2, 64, 256), bf16),
            pltpu.VMEM((4, 4, 2, 64, 256), bf16),
            pltpu.VMEM((2, 2, 4, 2) + piece, bf16),
            pltpu.VMEM((2, 2, 4, 2) + piece, bf16),
            pltpu.VMEM((2, 2, 4, 2) + piece, bf16),
            pltpu.VMEM((2, 2, 2) + piece, bf16),
            pltpu.VMEM((2, 2, 2) + piece, bf16),
            pltpu.VMEM((2, 2, 2) + piece, bf16),
            pltpu.VMEM((2, 2) + piece, bf16),
            pltpu.VMEM((2, 2) + piece, bf16),
            pltpu.VMEM((2, 2, 2) + piece, f32),
            pltpu.VMEM((2, 4, 4, 2, 2) + piece, bf16),
            pltpu.VMEM((2, rows, kv), f32),
            pltpu.VMEM((2, rows, kv), f32),
            pltpu.VMEM((2, 2, rows, kv // 2), bf16),
            pltpu.VMEM((2, 2, rows, kv // 2), bf16),
            pltpu.VMEM((tok, 2 * kv), f32),
            pltpu.VMEM((2, rows, kv), f32),
            pltpu.VMEM((2, rows, kv), f32),
            pltpu.VMEM((2, rows, kv), f32),
            pltpu.VMEM((2, rows, kv), f32),
            pltpu.SemaphoreType.DMA((28,)),
            pltpu.SemaphoreType.DMA((COUNT,)),
            pltpu.SemaphoreType.DMA((COUNT,)),
        ],
        compiler_params=pltpu.CompilerParams(
            collective_id=0, has_side_effects=True, vmem_limit_bytes=62 * 2**20
        ),
        cost_estimate=pl.CostEstimate(
            flops=17_200_000_000, bytes_accessed=16 * 2**20, transcendentals=0
        ),
        name="outer_step",
    )(
        activations, cotangent, first_moment[0], second_moment[0], inner_params[0],
        global_params, outer_momentum,
    )
    new_first, new_second, new_momentum, new_global = pl.pallas_call(
        hand_over,
        out_shape=(state,) * 4,
        in_specs=[anywhere] * 4,
        out_specs=(anywhere,) * 4,
        scratch_shapes=[held] * 4 + [pltpu.SemaphoreType.DMA((8,))],
        cost_estimate=pl.CostEstimate(flops=0, bytes_accessed=4 * 2**20, transcendentals=0),
        name="hand_over",
    )(*states)
    return (
        new_first[None], new_second[None], new_momentum, new_global,
        projected.reshape(tok, 2, kv),
    )


def solution(mesh):
    in_specs = (
        P(("island", "fsdp"), "tensor"),
        P(("island", "fsdp"), None, "tensor"),
        P("island", "fsdp", None, "tensor"),
        P("island", "fsdp", None, "tensor"),
        P("island", "fsdp", None, "tensor"),
        P("fsdp", None, "tensor"),
        P("fsdp", None, "tensor"),
    )
    out_specs = (
        P("island", "fsdp", None, "tensor"),
        P("island", "fsdp", None, "tensor"),
        P("fsdp", None, "tensor"),
        P("fsdp", None, "tensor"),
        P(("island", "fsdp"), None, "tensor"),
    )
    return jax.shard_map(shards, mesh=mesh, in_specs=in_specs, out_specs=out_specs, check_vma=False)
```
